512 devices in a mesh: section: 4 (over z_hi), seq: 32 (over x, y), head: 4 (over z_lo, core).
Axes of the slice: x: 4, y: 8, z: 8 (z_hi: 4, z_lo: 2; z = z_hi * 2 + z_lo), core: 2. Of those that a mesh axis runs over, the one named last changes fastest.
Arguments:
- lengths: int32 [4], replicated, may hold values from 1 to 3072, 4096 in all
- adapter: int32 [4], replicated, may hold values from 0 to 7
- query: bfloat16 [4, 4096, 1536], P('section', 'seq', 'head'), may hold values from -120 to 120
- previous_keys: bfloat16 [4, 4096, 1536], P('section', 'seq', 'head'), may hold values from -6 to 6
- previous_values: bfloat16 [4, 4096, 1536], P('section', 'seq', 'head'), may hold values from -6 to 6
- stream: bfloat16 [4, 4096, 3072], P('section', 'seq', 'head'), may hold values from -6 to 6
- gate: float32 [4, 4, 3072], P('section', None, 'head'), may hold values from 0.5 to 1.5
- output_matrix: bfloat16 [4, 1536, 3072], P('section', 'head'), may hold values from -0.15625 to 0.15625
- adapter_down: bfloat16 [4, 8, 1536, 64], P('section', None, 'head'), may hold values from -0.15625 to 0.15625
- adapter_up: bfloat16 [4, 8, 64, 3072], P('section', None, None, 'head'), may hold values from -0.75 to 0.75
Outputs:
- block_out: bfloat16 [4, 4096, 3072], P('section', 'seq', 'head')
The draws below stay inside these ranges and needn't reach their ends.
Inputs may be any that keep to these rules, and one draw needn't show every extreme that they name: `lengths`: the 4 counts fill all 4096 tokens in order; the largest is exactly 3072.
All inputs are finite; a program needn't handle non-finite values.
Results may differ from the reference program's by a relative error of at most 0.0075.
Values may be sent and summed in bfloat16 or wider, within the bound.
No kernel may reach another device: no remote copies, remote signals or barrier semaphores. Data moves between devices by JAX's collectives and lax.ppermute only.
A program may use at most 64 MiB of HBM per device.

```python
import math
import jax
import jax.numpy as jnp
import numpy as np
from jax import lax

MODEL_WIDTH = 3072
LOCAL_HEADS = 12
HEAD_SIZE = 128
ADAPTER_RANK = 64
ADAPTER_POOL = 8
REQS = 4
BATCH_TOKENS = 4096
N_SECTION = 4


def base_keys(key):
    full_shape = (N_SECTION, BATCH_TOKENS, LOCAL_HEADS * HEAD_SIZE)
    return jnp.clip(jax.random.normal(key, full_shape, jnp.float32), -5.0, 5.0)


def draw_query(key, part):
    key = jax.random.fold_in(key, 7)
    full_shape = (N_SECTION, BATCH_TOKENS, LOCAL_HEADS * HEAD_SIZE)
    drawn_rows = jnp.clip(jax.random.normal(key, full_shape, jnp.float32), -5.0, 5.0)
    return drawn_rows.astype(jnp.bfloat16)


def draw_previous_keys(key, part):
    base_rows = base_keys(key)
    return base_rows.astype(jnp.bfloat16)


def plant(entries, stream_key, low, top_value):
    longest = entries.shape.index(max(entries.shape))
    spots = []
    for shift in (0, 1):
        where = [jax.random.randint(jax.random.fold_in(stream_key, axis), (), 0, length) for axis, length in enumerate(entries.shape)]
        where[longest] = (where[longest] + shift) % entries.shape[longest]
        spots.append(tuple(where))
    return entries.at[spots[0]].set(low).at[spots[1]].set(top_value)


def levels(key, extent, shards, low, top_value):
    level = 1.0
    for dim, blocks in shards:
        draws = jax.random.uniform(jax.random.fold_in(jax.random.fold_in(key, 6), dim), (blocks,), jnp.float32, low / len(shards), top_value / len(shards))
        level = level * jnp.repeat(jnp.exp(draws), extent[dim] // blocks).reshape((-1,) + (1,) * (len(extent) - 1 - dim))
    return level


def length_profile(amount, total, reach, skew):
    portions = [(1 << 20) // math.isqrt(standing ** skew) + 1 for standing in range(2, amount + 1)]
    surplus, counts = total - reach - (amount - 1), [1] * (amount - 1)
    while surplus > 0:
        candidates = [i for i in range(amount - 1) if counts[i] < reach]
        whole, left = sum([portions[i] for i in candidates]), surplus
        for i in candidates:
            extra = min(reach - counts[i], max(1, left * portions[i] // whole), surplus)
            counts[i] = counts[i] + extra
            surplus = surplus - extra
    return np.array([reach] + counts)


def uneven_parts(key, amount, total, reach, skew):
    if amount == 2:
        one = jax.random.randint(key, (), max(1, total - reach), min(reach, total - 1) + 1)
        return jnp.stack([one, total - one])
    sizes = jnp.asarray(length_profile(amount, total, reach, skew), jnp.int32)
    twos = (amount - 1) // 2
    giver, sink = sizes[1:1 + 2 * twos:2], sizes[2:2 + 2 * twos:2]
    slack = jnp.minimum(giver - 1, reach - sink)
    moved = jax.random.randint(jax.random.fold_in(key, 1), (twos,), 0, 1 << 20) % (slack + 1)
    sizes = sizes.at[1:1 + 2 * twos:2].set(giver - moved).at[2:2 + 2 * twos:2].set(sink + moved)
    return sizes[jax.random.permutation(jax.random.fold_in(key, 2), amount)]


def bell_draw(rng, dims, scale, limit, split=(), held_as=jnp.bfloat16):
    drawn = scale * jax.random.normal(rng, dims, jnp.float32)
    if split:
        drawn = drawn * levels(rng, dims, split, -0.22, 0.18)
    return jnp.clip(drawn, -limit, limit).astype(held_as)


def setup_inputs(seed: int = 0) -> dict:
    arg_keys = jax.random.split(jax.random.key(seed), 11)
    lengths = uneven_parts(arg_keys[0], REQS, BATCH_TOKENS, BATCH_TOKENS - BATCH_TOKENS // 4, 2).astype(jnp.int32)
    adapter = plant(jax.random.randint(arg_keys[1], (REQS,), 0, ADAPTER_POOL), jax.random.fold_in(arg_keys[1], 1), 0, ADAPTER_POOL - 1).astype(jnp.int32)
    query = draw_query(jax.random.fold_in(arg_keys[10], 71), 0)
    previous_keys = draw_previous_keys(jax.random.fold_in(arg_keys[10], 71), 0)
    previous_values = bell_draw(arg_keys[4], (N_SECTION, BATCH_TOKENS, LOCAL_HEADS * HEAD_SIZE), 1.0, 6.0, ((0, 4), (1, 32), (2, 4)))
    stream = bell_draw(arg_keys[5], (N_SECTION, BATCH_TOKENS, MODEL_WIDTH), 1.0, 6.0, ((0, 4), (1, 32), (2, 4)))
    gate = jnp.clip(0.5 + 1.0 * jax.random.uniform(arg_keys[6], (N_SECTION, REQS, MODEL_WIDTH), jnp.float32) ** levels(arg_keys[6], (N_SECTION, REQS, MODEL_WIDTH), ((0, 4), (2, 4)), -0.2, 0.2), 0.5, 1.5)
    output_matrix = bell_draw(arg_keys[7], (N_SECTION, LOCAL_HEADS * HEAD_SIZE, MODEL_WIDTH), (LOCAL_HEADS * HEAD_SIZE) ** -0.5, 0.15625, ((0, 4), (1, 4)))
    adapter_down = bell_draw(arg_keys[8], (N_SECTION, ADAPTER_POOL, LOCAL_HEADS * HEAD_SIZE, ADAPTER_RANK), (LOCAL_HEADS * HEAD_SIZE) ** -0.5, 0.15625, ((0, 4), (2, 4)))
    adapter_up = bell_draw(arg_keys[9], (N_SECTION, ADAPTER_POOL, ADAPTER_RANK, MODEL_WIDTH), ADAPTER_RANK ** -0.5, 0.75, ((0, 4), (3, 4)))
    return {"lengths": lengths, "adapter": adapter, "query": query, "previous_keys": previous_keys, "previous_values": previous_values, "stream": stream, "gate": gate, "output_matrix": output_matrix, "adapter_down": adapter_down, "adapter_up": adapter_up}


NEG_FILL = -1e+30

def request_ids(lengths, count):
    request_ends = jnp.cumsum(lengths).astype(jnp.int32)
    position = jnp.arange(count, dtype=jnp.int32)
    hits = (position[:, None] >= request_ends[None, :]).astype(jnp.int32)
    return lax.optimization_barrier(jnp.sum(hits, axis=1)).astype(jnp.int32)

def attend_head(operands, segment):
    queries, keys, values = operands
    block_len = math.gcd(BATCH_TOKENS, 512)
    block_count = BATCH_TOKENS // block_len
    score_scale = 1.0 / math.sqrt(HEAD_SIZE)

    def one_block(block_item):
        query_rows, query_seg = block_item
        scores = jnp.dot(query_rows, keys.T, preferred_element_type=jnp.float32) * score_scale
        allowed = query_seg[:, None] == segment[None, :]
        scores = jnp.where(allowed, scores, NEG_FILL)
        row_max = lax.optimization_barrier(jnp.max(scores, axis=1, keepdims=True))
        weights = jnp.exp(scores - row_max)
        total = lax.optimization_barrier(jnp.sum(weights, axis=1, keepdims=True))
        numer = jnp.dot(weights.astype(jnp.bfloat16), values, preferred_element_type=jnp.float32)
        return (numer / total).astype(jnp.bfloat16)
    blocks = lax.map(one_block, (queries.reshape(block_count, block_len, HEAD_SIZE), segment.reshape(block_count, block_len)))
    return blocks.reshape(BATCH_TOKENS, HEAD_SIZE)

def reference(lengths, adapter, query, previous_keys, previous_values, stream, gate, output_matrix, adapter_down, adapter_up):
    segment = request_ids(lengths, BATCH_TOKENS)
    request_member = (segment[:, None] == jnp.arange(REQS, dtype=jnp.int32)[None, :]).astype(jnp.float32)
    received_state = jnp.roll(stream, 1, axis=0)
    results = []
    for section_index in range(query.shape[0]):
        head_q = query[section_index].reshape(BATCH_TOKENS, LOCAL_HEADS, HEAD_SIZE).transpose(1, 0, 2)
        head_k = previous_keys[section_index].reshape(BATCH_TOKENS, LOCAL_HEADS, HEAD_SIZE).transpose(1, 0, 2)
        head_v = previous_values[section_index].reshape(BATCH_TOKENS, LOCAL_HEADS, HEAD_SIZE).transpose(1, 0, 2)
        attn_heads = lax.map(lambda operands: attend_head(operands, segment), (head_q, head_k, head_v))
        attn = attn_heads.transpose(1, 0, 2).reshape(BATCH_TOKENS, LOCAL_HEADS * HEAD_SIZE)
        rank_middle = jnp.zeros((BATCH_TOKENS, ADAPTER_RANK), jnp.float32)
        for request_index in range(REQS):
            down_factor = adapter_down[section_index][adapter[request_index]]
            rank_middle = rank_middle + request_member[:, request_index:request_index + 1] * jnp.dot(attn, down_factor, preferred_element_type=jnp.float32)
        rank_middle = rank_middle.astype(jnp.bfloat16)
        adapter_term = jnp.zeros((BATCH_TOKENS, MODEL_WIDTH), jnp.float32)
        for request_index in range(REQS):
            up_factor = adapter_up[section_index][adapter[request_index]]
            adapter_term = adapter_term + request_member[:, request_index:request_index + 1] * jnp.dot(rank_middle, up_factor, preferred_element_type=jnp.float32)
        projected_rows = jnp.dot(attn, output_matrix[section_index], preferred_element_type=jnp.float32)
        gate_values = jnp.dot(request_member, gate[section_index], precision=lax.Precision.HIGHEST)
        final_output = received_state[section_index].astype(jnp.float32) + gate_values * (projected_rows + adapter_term)
        results.append(final_output.astype(jnp.bfloat16))
    return jnp.stack(results, axis=0)
```

```python
import functools
import math

import jax
import jax.numpy as jnp
from jax import lax
from jax.experimental import pallas as pl
from jax.experimental.pallas import tpu as pltpu
from jax.sharding import Mesh, PartitionSpec as P

HEAD = 128
NEG = -1e30
NX, NYH, NYL = 4, 4, 2
NZ, NC = 2, 2
STAT_ROWS = 16
F32 = jnp.float32
BF16 = jnp.bfloat16
VMEM_LIMIT = 48 * 1024 * 1024


def segment_of(position, info_ref, reqs):
    seg = jnp.zeros(position.shape, jnp.int32)
    for r in range(reqs):
        seg = seg + (position >= info_ref[r]).astype(jnp.int32)
    return seg


def attend_kernel(reqs, info_ref, q_ref, kv_ref, out_ref, kx_ref, vt_ref):
    rows = q_ref.shape[1]
    feats = q_ref.shape[2]
    heads = feats // HEAD
    keys = kv_ref.shape[0]
    step = pl.program_id(0)
    my_x, my_yh, my_yl = info_ref[reqs], info_ref[reqs + 1], info_ref[reqs + 2]
    scale = math.log2(math.e) / math.sqrt(HEAD)

    @pl.when(step == 0)
    def prepare():
        row = lax.broadcasted_iota(jnp.int32, (keys, HEAD), 0)
        lane = lax.broadcasted_iota(jnp.int32, (keys, HEAD), 1)
        block = row // rows
        place = ((my_x * NYH + block) * NYL + my_yl) * rows + (row - block * rows)
        seg = segment_of(place, info_ref, reqs)
        bar = jnp.where((lane < reqs) & (lane != seg), NEG, 0.0).astype(BF16)
        for h in range(heads):
            kx_ref[h, :, 0:HEAD] = kv_ref[:, h * HEAD : (h + 1) * HEAD]
            kx_ref[h, :, HEAD : 2 * HEAD] = bar
        vt_ref[...] = kv_ref[:, feats : 2 * feats].T

    n_q = NYL * rows
    first = (step * NYH + my_yh) * n_q
    place = first + lax.broadcasted_iota(jnp.int32, (n_q, HEAD), 0)
    lane = lax.broadcasted_iota(jnp.int32, (n_q, HEAD), 1)
    member = (segment_of(place, info_ref, reqs) == lane).astype(F32).astype(BF16)
    high, mid, low = [], [], []
    for h in range(heads):
        queries = q_ref[:, :, h * HEAD : (h + 1) * HEAD].reshape(n_q, HEAD)
        queries = jnp.concatenate([queries, member], axis=1)
        scores = lax.dot_general(kx_ref[h], queries, (((1,), (1,)), ((), ())), preferred_element_type=F32)
        top = jnp.max(scores, axis=0, keepdims=True)
        weights = jnp.exp2((scores - top) * scale)
        total = jnp.sum(weights, axis=0, keepdims=True)
        part = jnp.dot(vt_ref[h * HEAD : (h + 1) * HEAD, :], weights.astype(BF16), preferred_element_type=F32)
        part = (part * (1.0 / total)).astype(BF16)
        for i in range(NYL):
            out_ref[i, h * HEAD : (h + 1) * HEAD, :] = part[:, i * rows : (i + 1) * rows]
        level = top * scale + jnp.log2(total)
        a = level.astype(BF16).astype(F32)
        b = (level - a).astype(BF16).astype(F32)
        high.append(a)
        mid.append(b)
        low.append(level - a - b)
    blank = [jnp.zeros((1, n_q), F32)] * (STAT_ROWS - 3 * heads)
    stats = jnp.concatenate(high + mid + low + blank, axis=0).astype(BF16)
    for i in range(NYL):
        out_ref[i, feats : feats + STAT_ROWS, :] = stats[:, i * rows : (i + 1) * rows]


def project_kernel(reqs, info_ref, part_ref, down_ref, w_ref, send_ref, keep_ref):
    groups = part_ref.shape[0]
    feats, out_feats = w_ref.shape
    rows = part_ref.shape[2]
    heads = feats // HEAD
    quarter = out_feats // (NZ * NC)
    stat = part_ref[:, feats : feats + STAT_ROWS, :].astype(F32)
    level = stat[:, 0:heads] + stat[:, heads : 2 * heads] + stat[:, 2 * heads : 3 * heads]
    share = jnp.exp2(level - jnp.max(level, axis=0, keepdims=True))
    share = share / jnp.sum(share, axis=0, keepdims=True)
    columns = []
    for h in range(heads):
        acc = jnp.zeros((HEAD, rows), F32)
        for g in range(groups):
            acc = acc + part_ref[g, h * HEAD : (h + 1) * HEAD, :].astype(F32) * share[g, h : h + 1, :]
        columns.append(acc.T.astype(BF16))
    attn = jnp.concatenate(columns, axis=1)

    place = info_ref[2 * reqs] + lax.broadcasted_iota(jnp.int32, (rows, 1), 0)
    seg = segment_of(place, info_ref, reqs)
    rank = jnp.zeros((rows, down_ref.shape[2]), F32)
    for r in range(reqs):
        mid = jnp.dot(attn, down_ref[info_ref[reqs + r]], preferred_element_type=F32)
        rank = rank + jnp.where(seg == r, mid, 0.0)
    rank = jnp.concatenate([rank, jnp.zeros((rows, HEAD - rank.shape[1]), F32)], axis=1)
    core = info_ref[2 * reqs + 1]
    for z in range(NZ):
        for ref, c in ((send_ref, 1 - core), (keep_ref, core)):
            start = pl.multiple_of((z * NC + c) * quarter, quarter)
            product = jnp.dot(attn, w_ref[:, pl.ds(start, quarter)], preferred_element_type=F32)
            ref[:, z * quarter : (z + 1) * quarter] = product.astype(ref.dtype)
    send_ref[:, NZ * quarter : NZ * quarter + HEAD] = rank.astype(send_ref.dtype)
    keep_ref[:, NZ * quarter : NZ * quarter + HEAD] = rank.astype(keep_ref.dtype)


def finish_kernel(reqs, info_ref, mine_ref, other_ref, state_ref, gate_ref, up_ref, out_ref):
    rows, quarter = out_ref.shape
    ranks = up_ref.shape[1]
    place = info_ref[2 * reqs] + lax.broadcasted_iota(jnp.int32, (rows, 1), 0)
    seg = segment_of(place, info_ref, reqs)
    rank = mine_ref[:, quarter : quarter + ranks] + other_ref[:, quarter : quarter + ranks].astype(F32)
    rank = rank.astype(BF16)
    branch = mine_ref[:, 0:quarter] + other_ref[:, 0:quarter].astype(F32)
    gates = jnp.zeros((rows, quarter), F32)
    for r in range(reqs):
        chosen = jnp.where(seg == r, rank.astype(F32), 0.0).astype(BF16)
        branch = branch + jnp.dot(chosen, up_ref[info_ref[reqs + r]], preferred_element_type=F32)
        gates = jnp.where(seg == r, gate_ref[r : r + 1, :], gates)
    out_ref[...] = (state_ref[...].astype(F32) + gates * branch).astype(out_ref.dtype)


def shards(lengths, adapter, query, previous_keys, previous_values, stream, gate, output_matrix, adapter_down, adapter_up):
    rows, feats = query.shape[1:]
    reqs = lengths.shape[0]
    out_feats = output_matrix.shape[2]
    quarter = out_feats // (NZ * NC)
    group = NX * NYL
    my_x, my_yh, my_yl = lax.axis_index("x"), lax.axis_index("yh"), lax.axis_index("yl")
    my_z, my_core = lax.axis_index("zl"), lax.axis_index("core")
    ends = jnp.cumsum(lengths).astype(jnp.int32)
    first = ((my_x * NYH + my_yh) * NYL + my_yl) * rows
    info_attend = jnp.concatenate([ends, jnp.stack([my_x, my_yh, my_yl]).astype(jnp.int32)])
    info = jnp.concatenate([ends, adapter, jnp.stack([first, my_core]).astype(jnp.int32)])
    smem = pl.BlockSpec(memory_space=pltpu.SMEM)
    vmem = pl.BlockSpec(memory_space=pltpu.VMEM)
    params = pltpu.CompilerParams(vmem_limit_bytes=VMEM_LIMIT)

    sections = lax.axis_size("section")
    state = lax.ppermute(stream[0], "section", [(i, (i + 1) % sections) for i in range(sections)])

    queries = lax.all_to_all(jnp.broadcast_to(query, (group, rows, feats)), ("x", "yl"), 0, 0, tiled=True)
    kv = jnp.concatenate([previous_keys[0], previous_values[0]], axis=1)
    kv = lax.all_gather(kv, "yh", axis=0, tiled=True)

    keys = NYH * rows
    parts = pl.pallas_call(
        functools.partial(attend_kernel, reqs),
        grid=(NX,),
        in_specs=[
            smem,
            pl.BlockSpec((NYL, rows, feats), lambda i: (i, 0, 0)),
            pl.BlockSpec((keys, 2 * feats), lambda i: (0, 0)),
        ],
        out_specs=pl.BlockSpec((NYL, feats + STAT_ROWS, rows), lambda i: (i, 0, 0)),
        out_shape=jax.ShapeDtypeStruct((group, feats + STAT_ROWS, rows), BF16),
        scratch_shapes=[pltpu.VMEM((feats // HEAD, keys, 2 * HEAD), BF16), pltpu.VMEM((feats, keys), BF16)],
        compiler_params=params,
    )(info_attend, queries, kv)

    parts = lax.all_to_all(parts, ("x", "yl"), 0, 0, tiled=True)

    width = NZ * quarter + HEAD
    send, keep = pl.pallas_call(
        functools.partial(project_kernel, reqs),
        in_specs=[smem, vmem, vmem, vmem],
        out_specs=[vmem, vmem],
        out_shape=[jax.ShapeDtypeStruct((rows, width), BF16), jax.ShapeDtypeStruct((rows, width), F32)],
        compiler_params=params,
    )(info, parts, adapter_down[0], output_matrix[0])

    chip = keep + lax.ppermute(send, "core", [(0, 1), (1, 0)]).astype(F32)
    rank = chip[:, NZ * quarter :]
    here = lax.dynamic_slice_in_dim(chip, my_z * quarter, quarter, 1)
    there = lax.dynamic_slice_in_dim(chip, (1 - my_z) * quarter, quarter, 1)
    mine = jnp.concatenate([here, rank], axis=1)
    other = jnp.concatenate([there, rank], axis=1).astype(BF16)
    other = lax.ppermute(other, "zl", [(0, 1), (1, 0)])

    out = pl.pallas_call(
        functools.partial(finish_kernel, reqs),
        in_specs=[smem] + [vmem] * 5,
        out_specs=vmem,
        out_shape=jax.ShapeDtypeStruct((rows, quarter), BF16),
        compiler_params=params,
    )(info, mine, other, state, gate[0], adapter_up[0])
    return out[None]


def solution(mesh):
    devices = mesh.devices.reshape(mesh.shape["section"], NX, NYH, NYL, NZ, NC)
    fine = Mesh(devices, ("section", "x", "yh", "yl", "zl", "core"))
    seq, head = ("x", "yh", "yl"), ("zl", "core")
    placed = (
        P(),
        P(),
        P("section", seq, head),
        P("section", seq, head),
        P("section", seq, head),
        P("section", seq, head),
        P("section", None, head),
        P("section", head, None),
        P("section", None, head, None),
        P("section", None, None, head),
    )
    return jax.shard_map(shards, mesh=fine, in_specs=placed, out_specs=P("section", seq, head), check_vma=False)
```

```python
import functools
import math

import jax
import jax.numpy as jnp
from jax import lax
from jax.experimental import pallas as pl
from jax.experimental.pallas import tpu as pltpu
from jax.sharding import Mesh, PartitionSpec as P

HEAD = 128
NEG = -1e30
NX, NYH, NYL = 4, 4, 2
NZ, NC = 2, 2
STAT_ROWS = 16
F32 = jnp.float32
BF16 = jnp.bfloat16
VMEM_LIMIT = 48 * 1024 * 1024


def segment_of(position, lengths_ref):
    seg = jnp.zeros(position.shape, jnp.int32)
    end = 0
    for r in range(lengths_ref.shape[0]):
        end = end + lengths_ref[r]
        seg = seg + (position >= end).astype(jnp.int32)
    return seg


def own_segments(rows, lengths_ref):
    first = ((lax.axis_index("x") * NYH + lax.axis_index("yh")) * NYL + lax.axis_index("yl")) * rows
    return segment_of(first + lax.broadcasted_iota(jnp.int32, (rows, 1), 0), lengths_ref)


def spread_kernel(q_ref, out_ref):
    for i in range(out_ref.shape[0]):
        out_ref[i] = q_ref[...]


def attend_kernel(lengths_ref, q_ref, kv_ref, out_ref, kx_ref, vt_ref):
    reqs = lengths_ref.shape[0]
    blocks, rows, feats = out_ref.shape[0], out_ref.shape[2], q_ref.shape[1]
    heads = feats // HEAD
    keys = kv_ref.shape[0]
    my_x, my_yh, my_yl = lax.axis_index("x"), lax.axis_index("yh"), lax.axis_index("yl")
    scale = math.log2(math.e) / math.sqrt(HEAD)

    row = lax.broadcasted_iota(jnp.int32, (keys, HEAD), 0)
    lane = lax.broadcasted_iota(jnp.int32, (keys, HEAD), 1)
    block = row // rows
    place = ((my_x * NYH + block) * NYL + my_yl) * rows + (row - block * rows)
    seg = segment_of(place, lengths_ref)
    bar = jnp.where((lane < reqs) & (lane != seg), NEG, 0.0).astype(BF16)
    for h in range(heads):
        kx_ref[h, :, 0:HEAD] = kv_ref[:, h * HEAD : (h + 1) * HEAD]
        kx_ref[h, :, HEAD : 2 * HEAD] = bar
    vt_ref[...] = kv_ref[:, feats : 2 * feats].T

    n_q = blocks * rows
    span = NYL * rows
    row = lax.broadcasted_iota(jnp.int32, (n_q, HEAD), 0)
    lane = lax.broadcasted_iota(jnp.int32, (n_q, HEAD), 1)
    block = row // span
    place = (block * NYH + my_yh) * span + (row - block * span)
    member = (segment_of(place, lengths_ref) == lane).astype(F32).astype(BF16)
    scores = []
    for h in range(heads):
        queries = jnp.concatenate([q_ref[:, h * HEAD : (h + 1) * HEAD], member], axis=1)
        scores.append(lax.dot_general(kx_ref[h], queries, (((1,), (1,)), ((), ())), preferred_element_type=F32))
    tops = [jnp.max(s, axis=0, keepdims=True) for s in scores]
    weights, totals = [], []
    for h in range(heads):
        weight = jnp.exp2((scores[h] - tops[h]) * scale)
        totals.append(jnp.sum(weight, axis=0, keepdims=True))
        weights.append(weight.astype(BF16))
    high, mid, low = [], [], []
    for h in range(heads):
        part = jnp.dot(vt_ref[h * HEAD : (h + 1) * HEAD, :], weights[h], preferred_element_type=F32)
        part = (part * (1.0 / totals[h])).astype(BF16)
        for i in range(blocks):
            out_ref[i, h * HEAD : (h + 1) * HEAD, :] = part[:, i * rows : (i + 1) * rows]
        level = tops[h] * scale + jnp.log2(totals[h])
        a = level.astype(BF16).astype(F32)
        b = (level - a).astype(BF16).astype(F32)
        high.append(a)
        mid.append(b)
        low.append(level - a - b)
    blank = [jnp.zeros((1, n_q), F32)] * (STAT_ROWS - 3 * heads)
    stats = jnp.concatenate(high + mid + low + blank, axis=0).astype(BF16)
    for i in range(blocks):
        out_ref[i, feats : feats + STAT_ROWS, :] = stats[:, i * rows : (i + 1) * rows]


def project_kernel(lengths_ref, part_ref, down_ref, w_ref, send_ref, keep_ref):
    groups = part_ref.shape[0]
    feats, out_feats = w_ref.shape
    rows = part_ref.shape[2]
    heads = feats // HEAD
    quarter = out_feats // (NZ * NC)
    stat = part_ref[:, feats : feats + STAT_ROWS, :].astype(F32)
    level = stat[:, 0:heads] + stat[:, heads : 2 * heads] + stat[:, 2 * heads : 3 * heads]
    share = jnp.exp2(level - jnp.max(level, axis=0, keepdims=True))
    share = share / jnp.sum(share, axis=0, keepdims=True)
    columns = []
    for h in range(heads):
        acc = jnp.zeros((HEAD, rows), F32)
        for g in range(groups):
            acc = acc + part_ref[g, h * HEAD : (h + 1) * HEAD, :].astype(F32) * share[g, h : h + 1, :]
        columns.append(acc.T.astype(BF16))
    attn = jnp.concatenate(columns, axis=1)

    seg = own_segments(rows, lengths_ref)
    rank = jnp.zeros((rows, down_ref.shape[1]), F32)
    for r in range(lengths_ref.shape[0]):
        mid = lax.dot_general(attn, down_ref[r], (((1,), (1,)), ((), ())), preferred_element_type=F32)
        rank = rank + jnp.where(seg == r, mid, 0.0)
    rank = jnp.concatenate([rank, jnp.zeros((rows, HEAD - rank.shape[1]), F32)], axis=1)
    core = lax.axis_index("core")
    for z in range(NZ):
        for ref, c in ((send_ref, 1 - core), (keep_ref, core)):
            start = pl.multiple_of((z * NC + c) * quarter, quarter)
            product = jnp.dot(attn, w_ref[:, pl.ds(start, quarter)], preferred_element_type=F32)
            ref[:, z * quarter : (z + 1) * quarter] = product.astype(ref.dtype)
    send_ref[:, NZ * quarter : NZ * quarter + HEAD] = rank.astype(send_ref.dtype)
    keep_ref[:, NZ * quarter : NZ * quarter + HEAD] = rank.astype(keep_ref.dtype)


def hold_kernel(adapter_ref, matrix_ref, down_ref, w_ref, chosen_ref):
    w_ref[...] = matrix_ref[...]
    for r in range(chosen_ref.shape[0]):
        chosen_ref[r] = down_ref[adapter_ref[r]]


def fold_kernel(keep_ref, cores_ref, mine_ref, other_ref):
    quarter = mine_ref.shape[1] - HEAD
    core, z = lax.axis_index("core"), lax.axis_index("zl")
    for ref, which in ((other_ref, 1 - z), (mine_ref, z)):
        for cols, at in (
            (pl.ds(pl.multiple_of(which * quarter, quarter), quarter), pl.ds(0, quarter)),
            (pl.ds(NZ * quarter, HEAD), pl.ds(quarter, HEAD)),
        ):
            ref[:, at] = (keep_ref[:, cols] + cores_ref[1 - core, :, cols].astype(F32)).astype(ref.dtype)


def finish_kernel(lengths_ref, adapter_ref, mine_ref, other_ref, state_ref, gate_ref, up_ref, out_ref):
    rows, quarter = out_ref.shape
    ranks = up_ref.shape[1]
    seg = own_segments(rows, lengths_ref)
    there = 1 - lax.axis_index("zl")
    rank = mine_ref[:, quarter : quarter + ranks] + other_ref[there, :, quarter : quarter + ranks].astype(F32)
    rank = rank.astype(BF16).astype(F32)
    branch = mine_ref[:, 0:quarter] + other_ref[there, :, 0:quarter].astype(F32)
    gates = jnp.zeros((rows, quarter), F32)
    for r in range(lengths_ref.shape[0]):
        chosen = jnp.where(seg == r, rank, 0.0).astype(BF16)
        branch = branch + jnp.dot(chosen, up_ref[adapter_ref[r]], preferred_element_type=F32)
        gates = jnp.where(seg == r, gate_ref[r : r + 1, :], gates)
    out_ref[...] = (state_ref[...].astype(F32) + gates * branch).astype(out_ref.dtype)


def shards(lengths, adapter, query, previous_keys, previous_values, stream, gate, output_matrix, adapter_down, adapter_up):
    rows, feats = query.shape[1:]
    quarter = output_matrix.shape[2] // (NZ * NC)
    group = NX * NYL
    smem = pl.BlockSpec(memory_space=pltpu.SMEM)
    vmem = pl.BlockSpec(memory_space=pltpu.VMEM)
    hbm = pl.BlockSpec(memory_space=pl.ANY)
    params = pltpu.CompilerParams(vmem_limit_bytes=VMEM_LIMIT)

    sections = lax.axis_size("section")
    state = lax.ppermute(stream[0], "section", [(i, (i + 1) % sections) for i in range(sections)])

    pair = lax.all_gather(query[0], "yl", axis=0, tiled=True)
    queries = pl.pallas_call(
        spread_kernel,
        in_specs=[vmem],
        out_specs=vmem,
        out_shape=jax.ShapeDtypeStruct((NX, NYL * rows, feats), BF16),
        compiler_params=params,
    )(pair)
    kv = jnp.concatenate([previous_keys[0], previous_values[0]], axis=1)
    queries = lax.all_to_all(queries, "x", 0, 0, tiled=True)
    kv = lax.all_gather(kv, "yh", axis=0, tiled=True)

    keys = NYH * rows
    parts = pl.pallas_call(
        attend_kernel,
        in_specs=[smem, vmem, vmem],
        out_specs=vmem,
        out_shape=jax.ShapeDtypeStruct((group, feats + STAT_ROWS, rows), BF16),
        scratch_shapes=[pltpu.VMEM((feats // HEAD, keys, 2 * HEAD), BF16), pltpu.VMEM((feats, keys), BF16)],
        compiler_params=params,
    )(lengths, queries.reshape(group * rows, feats), kv)
    parts = lax.all_to_all(parts, ("x", "yl"), 0, 0, tiled=True)

    down = jnp.swapaxes(adapter_down[0], 1, 2)
    matrix, down = pl.pallas_call(
        hold_kernel,
        in_specs=[smem, vmem, vmem],
        out_specs=[vmem, vmem],
        out_shape=[
            jax.ShapeDtypeStruct(output_matrix.shape[1:], BF16),
            jax.ShapeDtypeStruct((adapter.shape[0],) + down.shape[1:], BF16),
        ],
        compiler_params=pltpu.CompilerParams(vmem_limit_bytes=32 * 1024 * 1024),
    )(adapter, output_matrix[0], down)
    width = NZ * quarter + HEAD
    send, keep = pl.pallas_call(
        project_kernel,
        in_specs=[smem, vmem, vmem, vmem],
        out_specs=[vmem, vmem],
        out_shape=[jax.ShapeDtypeStruct((rows, width), BF16), jax.ShapeDtypeStruct((rows, width), F32)],
        compiler_params=params,
    )(lengths, parts, down, matrix)
    cores = lax.all_gather(send, "core", axis=0, tiled=False)
    mine, other = pl.pallas_call(
        fold_kernel,
        in_specs=[vmem, vmem],
        out_specs=[vmem, vmem],
        out_shape=[jax.ShapeDtypeStruct((rows, quarter + HEAD), F32), jax.ShapeDtypeStruct((rows, quarter + HEAD), BF16)],
        compiler_params=params,
    )(keep, cores)
    other = lax.all_gather(other, "zl", axis=0, tiled=False)

    out = pl.pallas_call(
        finish_kernel,
        in_specs=[smem, smem] + [vmem] * 5,
        out_specs=vmem,
        out_shape=jax.ShapeDtypeStruct((rows, quarter), BF16),
        compiler_params=params,
    )(lengths, adapter, mine, other, state, gate[0], adapter_up[0])
    return out[None]


def solution(mesh):
    devices = mesh.devices.reshape(mesh.shape["section"], NX, NYH, NYL, NZ, NC)
    fine = Mesh(devices, ("section", "x", "yh", "yl", "zl", "core"))
    seq, head = ("x", "yh", "yl"), ("zl", "core")
    placed = (
        P(),
        P(),
        P("section", seq, head),
        P("section", seq, head),
        P("section", seq, head),
        P("section", seq, head),
        P("section", None, head),
        P("section", head, None),
        P("section", None, head, None),
        P("section", None, None, head),
    )
    return jax.shard_map(shards, mesh=fine, in_specs=placed, out_specs=P("section", seq, head), check_vma=False)
```

```python
import functools
import math

import jax
import jax.numpy as jnp
from jax import lax
from jax.experimental import pallas as pl
from jax.experimental.pallas import tpu as pltpu
from jax.sharding import Mesh, PartitionSpec as P

HEAD = 128
NEG = -1e30
NX, NYH, NYL = 4, 4, 2
NZ, NC = 2, 2
STAT_ROWS = 16
F32 = jnp.float32
BF16 = jnp.bfloat16
VMEM_LIMIT = 32 * 1024 * 1024


def segment_of(position, lengths_ref):
    seg = jnp.zeros(position.shape, jnp.int32)
    end = 0
    for r in range(lengths_ref.shape[0]):
        end = end + lengths_ref[r]
        seg = seg + (position >= end).astype(jnp.int32)
    return seg


def spans(lengths_ref):
    lane = lax.broadcasted_iota(jnp.int32, (1, HEAD), 1)
    start = jnp.zeros((1, HEAD), jnp.int32)
    stop = jnp.full((1, HEAD), jnp.iinfo(jnp.int32).max, jnp.int32)
    end = 0
    for r in range(lengths_ref.shape[0]):
        start = jnp.where(lane == r, end, start)
        end = end + lengths_ref[r]
        stop = jnp.where(lane == r, end, stop)
    return start, stop


def own_segments(rows, lengths_ref):
    first = ((lax.axis_index("x") * NYH + lax.axis_index("yh")) * NYL + lax.axis_index("yl")) * rows
    return segment_of(first + lax.broadcasted_iota(jnp.int32, (rows, 1), 0), lengths_ref)


def spread_kernel(q_ref, out_ref, sems):
    copies = [pltpu.make_async_copy(q_ref, out_ref.at[i], sems.at[i]) for i in range(out_ref.shape[0])]
    for copy in copies:
        copy.start()
    for copy in copies:
        copy.wait()


def attend_kernel(lengths_ref, q_ref, kv_ref, result_ref, vt_ref, out_ref, sems):
    blocks, rows, feats = out_ref.shape[0], out_ref.shape[2], q_ref.shape[1]
    heads = feats // HEAD
    keys = kv_ref.shape[0]
    my_x, my_yh, my_yl = lax.axis_index("x"), lax.axis_index("yh"), lax.axis_index("yl")
    scale = math.log2(math.e) / math.sqrt(HEAD)

    start, stop = spans(lengths_ref)
    row = lax.broadcasted_iota(jnp.int32, (keys, HEAD), 0)
    block = row // rows
    place = ((my_x * NYH + block) * NYL + my_yl) * rows + (row - block * rows)
    bar = jnp.where((place >= start) & (place < stop), 0.0, NEG).astype(BF16)
    vt_ref[...] = kv_ref[:, feats : 2 * feats].T

    n_q = blocks * rows
    span = NYL * rows
    row = lax.broadcasted_iota(jnp.int32, (n_q, HEAD), 0)
    block = row // span
    place = (block * NYH + my_yh) * span + (row - block * span)
    member = jnp.where((place >= start) & (place < stop), 1.0, 0.0).astype(BF16)
    scores = []
    for h in range(heads):
        at = slice(h * HEAD, (h + 1) * HEAD)
        these = jnp.concatenate([kv_ref[:, at], bar], axis=1)
        queries = jnp.concatenate([q_ref[:, at], member], axis=1)
        scores.append(lax.dot_general(these, queries, (((1,), (1,)), ((), ())), preferred_element_type=F32))
    copies = []

    def send(start, size):
        at = (slice(None), pl.ds(start, size))
        copies.append(pltpu.make_async_copy(out_ref.at[at], result_ref.at[at], sems.at[len(copies)]))
        copies[-1].start()

    high, mid, low = [], [], []
    for h in range(heads):
        top = jnp.max(scores[h], axis=0, keepdims=True)
        weight = jnp.exp2((scores[h] - top) * scale)
        total = jnp.sum(weight, axis=0, keepdims=True)
        part = jnp.dot(vt_ref[h * HEAD : (h + 1) * HEAD, :], weight.astype(BF16), preferred_element_type=F32)
        part = (part * (1.0 / total)).astype(BF16)
        for i in range(blocks):
            out_ref[i, h * HEAD : (h + 1) * HEAD, :] = part[:, i * rows : (i + 1) * rows]
        send(h * HEAD, HEAD)
        level = top * scale + jnp.log2(total)
        a = level.astype(BF16).astype(F32)
        b = (level - a).astype(BF16).astype(F32)
        high.append(a)
        mid.append(b)
        low.append(level - a - b)
    blank = [jnp.zeros((1, n_q), F32)] * (STAT_ROWS - 3 * heads)
    stats = jnp.concatenate(high + mid + low + blank, axis=0).astype(BF16)
    for i in range(blocks):
        out_ref[i, feats : feats + STAT_ROWS, :] = stats[:, i * rows : (i + 1) * rows]
    send(feats, STAT_ROWS)
    for copy in copies:
        copy.wait()


def project_kernel(lengths_ref, part_ref, down_ref, w_ref, send_ref, keep_ref):
    groups = part_ref.shape[0]
    feats, out_feats = w_ref.shape
    rows = part_ref.shape[2]
    heads = feats // HEAD
    quarter = out_feats // (NZ * NC)
    stat = part_ref[:, feats : feats + STAT_ROWS, :].astype(F32)
    level = stat[:, 0:heads] + stat[:, heads : 2 * heads] + stat[:, 2 * heads : 3 * heads]
    share = jnp.exp2(level - jnp.max(level, axis=0, keepdims=True))
    share = share / jnp.sum(share, axis=0, keepdims=True)
    columns = []
    for h in range(heads):
        acc = jnp.zeros((HEAD, rows), F32)
        for g in range(groups):
            acc = acc + part_ref[g, h * HEAD : (h + 1) * HEAD, :].astype(F32) * share[g, h : h + 1, :]
        columns.append(acc.T.astype(BF16))
    attn = jnp.concatenate(columns, axis=1)

    seg = own_segments(rows, lengths_ref)
    rank = jnp.zeros((rows, down_ref.shape[1]), F32)
    for r in range(lengths_ref.shape[0]):
        mid = lax.dot_general(attn, down_ref[r], (((1,), (1,)), ((), ())), preferred_element_type=F32)
        rank = rank + jnp.where(seg == r, mid, 0.0)
    rank = jnp.concatenate([rank] * (HEAD // rank.shape[1]), axis=1)
    core = lax.axis_index("core")
    for z in range(NZ):
        for ref, c in ((send_ref, 1 - core), (keep_ref, core)):
            start = pl.multiple_of((z * NC + c) * quarter, quarter)
            product = jnp.dot(attn, w_ref[:, pl.ds(start, quarter)], preferred_element_type=F32)
            ref[:, z * quarter : (z + 1) * quarter] = product.astype(ref.dtype)
    send_ref[:, NZ * quarter : NZ * quarter + HEAD] = rank.astype(send_ref.dtype)
    keep_ref[:, NZ * quarter : NZ * quarter + HEAD] = rank.astype(keep_ref.dtype)


def hold_kernel(adapter_ref, matrix_ref, down_ref, w_ref, chosen_ref):
    w_ref[...] = matrix_ref[...]
    for r in range(chosen_ref.shape[0]):
        chosen_ref[r] = down_ref[adapter_ref[r]]


def fold_kernel(keep_ref, cores_ref, mine_ref, other_ref):
    quarter = mine_ref.shape[1] - HEAD
    core, z = lax.axis_index("core"), lax.axis_index("zl")
    for ref, which in ((other_ref, 1 - z), (mine_ref, z)):
        for cols, at in (
            (pl.ds(pl.multiple_of(which * quarter, quarter), quarter), pl.ds(0, quarter)),
            (pl.ds(NZ * quarter, HEAD), pl.ds(quarter, HEAD)),
        ):
            ref[:, at] = (keep_ref[:, cols] + cores_ref[1 - core, :, cols].astype(F32)).astype(ref.dtype)


def finish_kernel(lengths_ref, adapter_ref, mine_ref, other_ref, state_ref, gate_ref, up_ref, out_ref):
    rows, quarter = out_ref.shape
    reqs = lengths_ref.shape[0]
    ranks = up_ref.shape[1]
    seg = own_segments(rows, lengths_ref)
    there = 1 - lax.axis_index("zl")
    rank = mine_ref[:, quarter : quarter + HEAD] + other_ref[there, :, quarter : quarter + HEAD].astype(F32)
    rank = jnp.concatenate([rank] * (reqs * ranks // HEAD), axis=1)
    owner = lax.broadcasted_iota(jnp.int32, rank.shape, 1) // ranks
    rank = jnp.where(seg == owner, rank, 0.0).astype(BF16)
    ups = jnp.concatenate([up_ref[adapter_ref[r]] for r in range(reqs)], axis=0)
    gates = jnp.zeros((rows, quarter), F32)
    for r in range(reqs):
        gates = jnp.where(seg == r, gate_ref[r : r + 1, :], gates)
    branch = mine_ref[:, 0:quarter] + other_ref[there, :, 0:quarter].astype(F32)
    branch = branch + jnp.dot(rank, ups, preferred_element_type=F32)
    out_ref[...] = (state_ref[...].astype(F32) + gates * branch).astype(out_ref.dtype)


def shards(lengths, adapter, query, previous_keys, previous_values, stream, gate, output_matrix, adapter_down, adapter_up):
    rows, feats = query.shape[1:]
    quarter = output_matrix.shape[2] // (NZ * NC)
    group = NX * NYL
    smem = pl.BlockSpec(memory_space=pltpu.SMEM)
    vmem = pl.BlockSpec(memory_space=pltpu.VMEM)
    hbm = pl.BlockSpec(memory_space=pl.ANY)
    params = pltpu.CompilerParams(vmem_limit_bytes=VMEM_LIMIT)

    sections = lax.axis_size("section")
    state = lax.ppermute(stream[0], "section", [(i, (i + 1) % sections) for i in range(sections)])

    pair = lax.all_gather(query[0], "yl", axis=0, tiled=True)
    queries = pl.pallas_call(
        spread_kernel,
        in_specs=[vmem],
        out_specs=hbm,
        out_shape=jax.ShapeDtypeStruct((NX, NYL * rows, feats), BF16),
        scratch_shapes=[pltpu.SemaphoreType.DMA((NX,))],
        compiler_params=params,
    )(pair)
    kv = jnp.concatenate([previous_keys[0], previous_values[0]], axis=1)
    queries = lax.all_to_all(queries, "x", 0, 0, tiled=True)
    kv = lax.all_gather(kv, "yh", axis=0, tiled=True)

    keys = NYH * rows
    parts = pl.pallas_call(
        attend_kernel,
        in_specs=[smem, vmem, vmem],
        out_specs=hbm,
        out_shape=jax.ShapeDtypeStruct((group, feats + STAT_ROWS, rows), BF16),
        scratch_shapes=[
            pltpu.VMEM((feats, keys), BF16),
            pltpu.VMEM((group, feats + STAT_ROWS, rows), BF16),
            pltpu.SemaphoreType.DMA((feats // HEAD + 1,)),
        ],
        compiler_params=params,
    )(lengths, queries.reshape(group * rows, feats), kv)
    parts = lax.all_to_all(parts, ("x", "yl"), 0, 0, tiled=True)

    down = jnp.swapaxes(adapter_down[0], 1, 2)
    matrix, down = pl.pallas_call(
        hold_kernel,
        in_specs=[smem, vmem, vmem],
        out_specs=[vmem, vmem],
        out_shape=[
            jax.ShapeDtypeStruct(output_matrix.shape[1:], BF16),
            jax.ShapeDtypeStruct((adapter.shape[0],) + down.shape[1:], BF16),
        ],
        compiler_params=pltpu.CompilerParams(vmem_limit_bytes=VMEM_LIMIT),
    )(adapter, output_matrix[0], down)
    width = NZ * quarter + HEAD
    send, keep = pl.pallas_call(
        project_kernel,
        in_specs=[smem, vmem, vmem, vmem],
        out_specs=[vmem, vmem],
        out_shape=[jax.ShapeDtypeStruct((rows, width), BF16), jax.ShapeDtypeStruct((rows, width), F32)],
        compiler_params=params,
    )(lengths, parts, down, matrix)
    cores = lax.all_gather(send, "core", axis=0, tiled=False)
    mine, other = pl.pallas_call(
        fold_kernel,
        in_specs=[vmem, vmem],
        out_specs=[vmem, vmem],
        out_shape=[jax.ShapeDtypeStruct((rows, quarter + HEAD), F32), jax.ShapeDtypeStruct((rows, quarter + HEAD), BF16)],
        compiler_params=params,
    )(keep, cores)
    other = lax.all_gather(other, "zl", axis=0, tiled=False)

    out = pl.pallas_call(
        finish_kernel,
        in_specs=[smem, smem] + [vmem] * 5,
        out_specs=vmem,
        out_shape=jax.ShapeDtypeStruct((rows, quarter), BF16),
        compiler_params=params,
    )(lengths, adapter, mine, other, state, gate[0], adapter_up[0])
    return out[None]


def solution(mesh):
    devices = mesh.devices.reshape(mesh.shape["section"], NX, NYH, NYL, NZ, NC)
    fine = Mesh(devices, ("section", "x", "yh", "yl", "zl", "core"))
    seq, head = ("x", "yh", "yl"), ("zl", "core")
    placed = (
        P(),
        P(),
        P("section", seq, head),
        P("section", seq, head),
        P("section", seq, head),
        P("section", seq, head),
        P("section", None, head),
        P("section", head, None),
        P("section", None, head, None),
        P("section", None, None, head),
    )
    return jax.shard_map(shards, mesh=fine, in_specs=placed, out_specs=P("section", seq, head), check_vma=False)
```

```python
import functools
import math

import jax
import jax.numpy as jnp
from jax import lax
from jax.experimental import pallas as pl
from jax.experimental.pallas import tpu as pltpu
from jax.sharding import Mesh, PartitionSpec as P

HEAD = 128
NEG = -1e30
NX, NYH, NYL = 4, 4, 2
NZ, NC = 2, 2
STAT_ROWS = 16
F32 = jnp.float32
BF16 = jnp.bfloat16
VMEM_LIMIT = 32 * 1024 * 1024


def segment_of(position, lengths_ref):
    seg = jnp.zeros(position.shape, jnp.int32)
    end = 0
    for r in range(lengths_ref.shape[0]):
        end = end + lengths_ref[r]
        seg = seg + (position >= end).astype(jnp.int32)
    return seg


def spans(lengths_ref):
    lane = lax.broadcasted_iota(jnp.int32, (1, HEAD), 1)
    start = jnp.zeros((1, HEAD), jnp.int32)
    stop = jnp.full((1, HEAD), jnp.iinfo(jnp.int32).max, jnp.int32)
    end = 0
    for r in range(lengths_ref.shape[0]):
        start = jnp.where(lane == r, end, start)
        end = end + lengths_ref[r]
        stop = jnp.where(lane == r, end, stop)
    return start, stop


def own_segments(rows, lengths_ref):
    first = ((lax.axis_index("x") * NYH + lax.axis_index("yh")) * NYL + lax.axis_index("yl")) * rows
    return segment_of(first + lax.broadcasted_iota(jnp.int32, (rows, 1), 0), lengths_ref)


def spread_kernel(q_ref, out_ref, sems):
    copies = [pltpu.make_async_copy(q_ref, out_ref.at[i], sems.at[i]) for i in range(out_ref.shape[0])]
    for copy in copies:
        copy.start()
    for copy in copies:
        copy.wait()


def attend_kernel(lengths_ref, q_ref, kv_ref, result_ref, vt_ref, out_ref, sems):
    blocks, rows, feats = out_ref.shape[0], out_ref.shape[2], q_ref.shape[1]
    heads = feats // HEAD
    keys = kv_ref.shape[0]
    my_x, my_yh, my_yl = lax.axis_index("x"), lax.axis_index("yh"), lax.axis_index("yl")
    scale = math.log2(math.e) / math.sqrt(HEAD)

    start, stop = spans(lengths_ref)
    row = lax.broadcasted_iota(jnp.int32, (keys, HEAD), 0)
    block = row // rows
    place = ((my_x * NYH + block) * NYL + my_yl) * rows + (row - block * rows)
    bar = jnp.where((place >= start) & (place < stop), 0.0, NEG).astype(BF16)
    vt_ref[...] = kv_ref[:, feats : 2 * feats].T

    n_q = blocks * rows
    span = NYL * rows
    row = lax.broadcasted_iota(jnp.int32, (n_q, HEAD), 0)
    block = row // span
    place = (block * NYH + my_yh) * span + (row - block * span)
    member = jnp.where((place >= start) & (place < stop), 1.0, 0.0).astype(BF16)
    scores = []
    for h in range(heads):
        at = slice(h * HEAD, (h + 1) * HEAD)
        these = jnp.concatenate([kv_ref[:, at], bar], axis=1)
        queries = jnp.concatenate([q_ref[:, at], member], axis=1)
        scores.append(lax.dot_general(these, queries, (((1,), (1,)), ((), ())), preferred_element_type=F32))
    copies = []

    def send(start, size):
        at = (slice(None), pl.ds(start, size))
        copies.append(pltpu.make_async_copy(out_ref.at[at], result_ref.at[at], sems.at[len(copies)]))
        copies[-1].start()

    high, mid, low = [], [], []
    for h in range(heads):
        top = jnp.max(scores[h], axis=0, keepdims=True)
        weight = jnp.exp2((scores[h] - top) * scale)
        total = jnp.sum(weight, axis=0, keepdims=True)
        part = jnp.dot(vt_ref[h * HEAD : (h + 1) * HEAD, :], weight.astype(BF16), preferred_element_type=F32)
        part = (part * (1.0 / total)).astype(BF16)
        for i in range(blocks):
            out_ref[(i % NYL) * NX + i // NYL, h * HEAD : (h + 1) * HEAD, :] = part[:, i * rows : (i + 1) * rows]
        send(h * HEAD, HEAD)
        level = top * scale + jnp.log2(total)
        a = level.astype(BF16).astype(F32)
        b = (level - a).astype(BF16).astype(F32)
        high.append(a)
        mid.append(b)
        low.append(level - a - b)
    blank = [jnp.zeros((1, n_q), F32)] * (STAT_ROWS - 3 * heads)
    stats = jnp.concatenate(high + mid + low + blank, axis=0).astype(BF16)
    for i in range(blocks):
        out_ref[(i % NYL) * NX + i // NYL, feats : feats + STAT_ROWS, :] = stats[:, i * rows : (i + 1) * rows]
    send(feats, STAT_ROWS)
    for copy in copies:
        copy.wait()


def project_kernel(lengths_ref, part_ref, down_ref, w_ref, send_ref, keep_ref):
    groups = part_ref.shape[0]
    feats, out_feats = w_ref.shape
    rows = part_ref.shape[2]
    heads = feats // HEAD
    quarter = out_feats // (NZ * NC)
    stat = part_ref[:, feats : feats + STAT_ROWS, :].astype(F32)
    level = stat[:, 0:heads] + stat[:, heads : 2 * heads] + stat[:, 2 * heads : 3 * heads]
    share = jnp.exp2(level - jnp.max(level, axis=0, keepdims=True))
    share = share / jnp.sum(share, axis=0, keepdims=True)
    columns = []
    for h in range(heads):
        acc = jnp.zeros((HEAD, rows), F32)
        for g in range(groups):
            acc = acc + part_ref[g, h * HEAD : (h + 1) * HEAD, :].astype(F32) * share[g, h : h + 1, :]
        columns.append(acc.T.astype(BF16))
    attn = jnp.concatenate(columns, axis=1)

    seg = own_segments(rows, lengths_ref)
    rank = jnp.zeros((rows, down_ref.shape[1]), F32)
    for r in range(lengths_ref.shape[0]):
        mid = lax.dot_general(attn, down_ref[r], (((1,), (1,)), ((), ())), preferred_element_type=F32)
        rank = rank + jnp.where(seg == r, mid, 0.0)
    rank = jnp.concatenate([rank] * (HEAD // rank.shape[1]), axis=1)
    core = lax.axis_index("core")
    for z in range(NZ):
        for ref, c in ((send_ref, 1 - core), (keep_ref, core)):
            start = pl.multiple_of((z * NC + c) * quarter, quarter)
            product = jnp.dot(attn, w_ref[:, pl.ds(start, quarter)], preferred_element_type=F32)
            ref[:, z * quarter : (z + 1) * quarter] = product.astype(ref.dtype)
    send_ref[:, NZ * quarter : NZ * quarter + HEAD] = rank.astype(send_ref.dtype)
    keep_ref[:, NZ * quarter : NZ * quarter + HEAD] = rank.astype(keep_ref.dtype)


def hold_kernel(adapter_ref, matrix_ref, down_ref, w_ref, chosen_ref):
    w_ref[...] = matrix_ref[...]
    for r in range(chosen_ref.shape[0]):
        chosen_ref[r] = down_ref[adapter_ref[r]]


def fold_kernel(keep_ref, cores_ref, mine_ref, other_ref):
    quarter = mine_ref.shape[1] - HEAD
    core, z = lax.axis_index("core"), lax.axis_index("zl")
    for ref, which in ((other_ref, 1 - z), (mine_ref, z)):
        for cols, at in (
            (pl.ds(pl.multiple_of(which * quarter, quarter), quarter), pl.ds(0, quarter)),
            (pl.ds(NZ * quarter, HEAD), pl.ds(quarter, HEAD)),
        ):
            ref[:, at] = (keep_ref[:, cols] + cores_ref[1 - core, :, cols].astype(F32)).astype(ref.dtype)


def finish_kernel(lengths_ref, adapter_ref, mine_ref, other_ref, state_ref, gate_ref, up_ref, out_ref):
    rows, quarter = out_ref.shape
    reqs = lengths_ref.shape[0]
    ranks = up_ref.shape[1]
    seg = own_segments(rows, lengths_ref)
    there = 1 - lax.axis_index("zl")
    rank = mine_ref[:, quarter : quarter + HEAD] + other_ref[there, :, quarter : quarter + HEAD].astype(F32)
    rank = jnp.concatenate([rank] * (reqs * ranks // HEAD), axis=1)
    owner = lax.broadcasted_iota(jnp.int32, rank.shape, 1) // ranks
    rank = jnp.where(seg == owner, rank, 0.0).astype(BF16)
    ups = jnp.concatenate([up_ref[adapter_ref[r]] for r in range(reqs)], axis=0)
    gates = jnp.zeros((rows, quarter), F32)
    for r in range(reqs):
        gates = jnp.where(seg == r, gate_ref[r : r + 1, :], gates)
    branch = mine_ref[:, 0:quarter] + other_ref[there, :, 0:quarter].astype(F32)
    branch = branch + jnp.dot(rank, ups, preferred_element_type=F32)
    out_ref[...] = (state_ref[...].astype(F32) + gates * branch).astype(out_ref.dtype)


def shards(lengths, adapter, query, previous_keys, previous_values, stream, gate, output_matrix, adapter_down, adapter_up):
    rows, feats = query.shape[1:]
    quarter = output_matrix.shape[2] // (NZ * NC)
    group = NX * NYL
    smem = pl.BlockSpec(memory_space=pltpu.SMEM)
    vmem = pl.BlockSpec(memory_space=pltpu.VMEM)
    hbm = pl.BlockSpec(memory_space=pl.ANY)
    params = pltpu.CompilerParams(vmem_limit_bytes=VMEM_LIMIT)

    sections = lax.axis_size("section")
    state = lax.ppermute(stream[0], "section", [(i, (i + 1) % sections) for i in range(sections)])

    pair = lax.all_gather(query[0], "yl", axis=0, tiled=True)
    queries = pl.pallas_call(
        spread_kernel,
        in_specs=[vmem],
        out_specs=hbm,
        out_shape=jax.ShapeDtypeStruct((NX, NYL * rows, feats), BF16),
        scratch_shapes=[pltpu.SemaphoreType.DMA((NX,))],
        compiler_params=params,
    )(pair)
    kv = jnp.concatenate([previous_keys[0], previous_values[0]], axis=1)
    queries = lax.all_to_all(queries, "x", 0, 0, tiled=True)
    kv = lax.all_gather(kv, "yh", axis=0, tiled=True)

    keys = NYH * rows
    parts = pl.pallas_call(
        attend_kernel,
        in_specs=[smem, vmem, vmem],
        out_specs=hbm,
        out_shape=jax.ShapeDtypeStruct((group, feats + STAT_ROWS, rows), BF16),
        scratch_shapes=[
            pltpu.VMEM((feats, keys), BF16),
            pltpu.VMEM((group, feats + STAT_ROWS, rows), BF16),
            pltpu.SemaphoreType.DMA((feats // HEAD + 1,)),
        ],
        compiler_params=params,
    )(lengths, queries.reshape(group * rows, feats), kv)
    parts = lax.all_to_all(parts, ("yl", "x"), 0, 0, tiled=True)

    down = jnp.swapaxes(adapter_down[0], 1, 2)
    matrix, down = pl.pallas_call(
        hold_kernel,
        in_specs=[smem, vmem, vmem],
        out_specs=[vmem, vmem],
        out_shape=[
            jax.ShapeDtypeStruct(output_matrix.shape[1:], BF16),
            jax.ShapeDtypeStruct((adapter.shape[0],) + down.shape[1:], BF16),
        ],
        compiler_params=pltpu.CompilerParams(vmem_limit_bytes=VMEM_LIMIT),
    )(adapter, output_matrix[0], down)
    width = NZ * quarter + HEAD
    send, keep = pl.pallas_call(
        project_kernel,
        in_specs=[smem, vmem, vmem, vmem],
        out_specs=[vmem, vmem],
        out_shape=[jax.ShapeDtypeStruct((rows, width), BF16), jax.ShapeDtypeStruct((rows, width), F32)],
        compiler_params=params,
    )(lengths, parts, down, matrix)
    cores = lax.all_gather(send, "core", axis=0, tiled=False)
    mine, other = pl.pallas_call(
        fold_kernel,
        in_specs=[vmem, vmem],
        out_specs=[vmem, vmem],
        out_shape=[jax.ShapeDtypeStruct((rows, quarter + HEAD), F32), jax.ShapeDtypeStruct((rows, quarter + HEAD), BF16)],
        compiler_params=params,
    )(keep, cores)
    other = lax.all_gather(other, "zl", axis=0, tiled=False)

    out = pl.pallas_call(
        finish_kernel,
        in_specs=[smem, smem] + [vmem] * 5,
        out_specs=vmem,
        out_shape=jax.ShapeDtypeStruct((rows, quarter), BF16),
        compiler_params=params,
    )(lengths, adapter, mine, other, state, gate[0], adapter_up[0])
    return out[None]


def solution(mesh):
    devices = mesh.devices.reshape(mesh.shape["section"], NX, NYH, NYL, NZ, NC)
    fine = Mesh(devices, ("section", "x", "yh", "yl", "zl", "core"))
    seq, head = ("x", "yh", "yl"), ("zl", "core")
    placed = (
        P(),
        P(),
        P("section", seq, head),
        P("section", seq, head),
        P("section", seq, head),
        P("section", seq, head),
        P("section", None, head),
        P("section", head, None),
        P("section", None, head, None),
        P("section", None, None, head),
    )
    return jax.shard_map(shards, mesh=fine, in_specs=placed, out_specs=P("section", seq, head), check_vma=False)
```

```python
import functools
import math

import jax
import jax.numpy as jnp
from jax import lax
from jax.experimental import pallas as pl
from jax.experimental.pallas import tpu as pltpu
from jax.sharding import Mesh, PartitionSpec as P

HEAD = 128
NEG = -1e30
NX, NYH, NYL = 4, 4, 2
NZ, NC = 2, 2
STAT_ROWS = 16
ORDER = [0, 4, 2, 6, 1, 5, 3, 7]
F32 = jnp.float32
BF16 = jnp.bfloat16
VMEM_LIMIT = 16 * 1024 * 1024


def segment_of(position, lengths_ref):
    seg = jnp.zeros(position.shape, jnp.int32)
    end = 0
    for r in range(lengths_ref.shape[0]):
        end = end + lengths_ref[r]
        seg = seg + (position >= end).astype(jnp.int32)
    return seg


def spans(lengths_ref):
    lane = lax.broadcasted_iota(jnp.int32, (1, HEAD), 1)
    start = jnp.zeros((1, HEAD), jnp.int32)
    stop = jnp.full((1, HEAD), jnp.iinfo(jnp.int32).max, jnp.int32)
    end = 0
    for r in range(lengths_ref.shape[0]):
        start = jnp.where(lane == r, end, start)
        end = end + lengths_ref[r]
        stop = jnp.where(lane == r, end, stop)
    return start, stop


def own_segments(rows, lengths_ref):
    first = ((lax.axis_index("x") * NYH + lax.axis_index("yh")) * NYL + lax.axis_index("yl")) * rows
    return segment_of(first + lax.broadcasted_iota(jnp.int32, (rows, 1), 0), lengths_ref)


def spread_kernel(q_ref, out_ref, sems):
    copies = [pltpu.make_async_copy(q_ref, out_ref.at[i], sems.at[i]) for i in range(out_ref.shape[0])]
    for copy in copies:
        copy.start()
    for copy in copies:
        copy.wait()


def attend_kernel(lengths_ref, q_ref, kv_ref, result_ref, vt_ref, out_ref, sems):
    blocks, rows, feats = out_ref.shape[0], out_ref.shape[2], q_ref.shape[1]
    heads = feats // HEAD
    keys = kv_ref.shape[0]
    my_x, my_yh, my_yl = lax.axis_index("x"), lax.axis_index("yh"), lax.axis_index("yl")
    scale = math.log2(math.e) / math.sqrt(HEAD)

    start, stop = spans(lengths_ref)
    row = lax.broadcasted_iota(jnp.int32, (keys, HEAD), 0)
    block = row // rows
    place = ((my_x * NYH + block) * NYL + my_yl) * rows + (row - block * rows)
    bar = jnp.where((place >= start) & (place < stop), 0.0, NEG).astype(BF16)
    vt_ref[...] = kv_ref[:, feats : 2 * feats].T

    n_q = blocks * rows
    span = NYL * rows
    row = lax.broadcasted_iota(jnp.int32, (n_q, HEAD), 0)
    block = row // span
    place = (block * NYH + my_yh) * span + (row - block * span)
    member = jnp.where((place >= start) & (place < stop), 1.0, 0.0).astype(BF16)
    scores = []
    for h in range(heads):
        at = slice(h * HEAD, (h + 1) * HEAD)
        these = jnp.concatenate([kv_ref[:, at], bar], axis=1)
        queries = jnp.concatenate([q_ref[:, at], member], axis=1)
        scores.append(lax.dot_general(these, queries, (((1,), (1,)), ((), ())), preferred_element_type=F32))
    copies = []

    def send(start, size):
        at = (slice(None), pl.ds(start, size))
        copies.append(pltpu.make_async_copy(out_ref.at[at], result_ref.at[at], sems.at[len(copies)]))
        copies[-1].start()

    high, mid, low = [], [], []
    for h in range(heads):
        top = jnp.max(scores[h], axis=0, keepdims=True)
        weight = jnp.exp2((scores[h] - top) * scale)
        total = jnp.sum(weight, axis=0, keepdims=True)
        part = jnp.dot(vt_ref[h * HEAD : (h + 1) * HEAD, :], weight.astype(BF16), preferred_element_type=F32)
        part = (part * (1.0 / total)).astype(BF16)
        for i in range(blocks):
            out_ref[ORDER.index(i), h * HEAD : (h + 1) * HEAD, :] = part[:, i * rows : (i + 1) * rows]
        send(h * HEAD, HEAD)
        level = top * scale + jnp.log2(total)
        a = level.astype(BF16).astype(F32)
        b = (level - a).astype(BF16).astype(F32)
        high.append(a)
        mid.append(b)
        low.append(level - a - b)
    blank = [jnp.zeros((1, n_q), F32)] * (STAT_ROWS - 3 * heads)
    stats = jnp.concatenate(high + mid + low + blank, axis=0).astype(BF16)
    for i in range(blocks):
        out_ref[ORDER.index(i), feats : feats + STAT_ROWS, :] = stats[:, i * rows : (i + 1) * rows]
    send(feats, STAT_ROWS)
    for copy in copies:
        copy.wait()


def project_kernel(lengths_ref, part_ref, down_ref, w_ref, send_ref, keep_ref):
    groups = part_ref.shape[0]
    feats, out_feats = w_ref.shape
    rows = part_ref.shape[2]
    heads = feats // HEAD
    quarter = out_feats // (NZ * NC)
    stat = part_ref[:, feats : feats + STAT_ROWS, :].astype(F32)
    level = stat[:, 0:heads] + stat[:, heads : 2 * heads] + stat[:, 2 * heads : 3 * heads]
    share = jnp.exp2(level - jnp.max(level, axis=0, keepdims=True))
    share = share / jnp.sum(share, axis=0, keepdims=True)
    columns = []
    for h in range(heads):
        acc = jnp.zeros((HEAD, rows), F32)
        for g in range(groups):
            acc = acc + part_ref[g, h * HEAD : (h + 1) * HEAD, :].astype(F32) * share[g, h : h + 1, :]
        columns.append(acc.T.astype(BF16))
    attn = jnp.concatenate(columns, axis=1)

    seg = own_segments(rows, lengths_ref)
    rank = jnp.zeros((rows, down_ref.shape[1]), F32)
    for r in range(lengths_ref.shape[0]):
        mid = lax.dot_general(attn, down_ref[r], (((1,), (1,)), ((), ())), preferred_element_type=F32)
        rank = rank + jnp.where(seg == r, mid, 0.0)
    rank = jnp.concatenate([rank] * (HEAD // rank.shape[1]), axis=1)
    core = lax.axis_index("core")
    for z in range(NZ):
        for ref, c in ((send_ref, 1 - core), (keep_ref, core)):
            start = pl.multiple_of((z * NC + c) * quarter, quarter)
            product = jnp.dot(attn, w_ref[:, pl.ds(start, quarter)], preferred_element_type=F32)
            ref[:, z * quarter : (z + 1) * quarter] = product.astype(ref.dtype)
    send_ref[:, NZ * quarter : NZ * quarter + HEAD] = rank.astype(send_ref.dtype)
    keep_ref[:, NZ * quarter : NZ * quarter + HEAD] = rank.astype(keep_ref.dtype)


def hold_kernel(matrix_ref, w_ref):
    w_ref[...] = matrix_ref[...]


def choose_kernel(adapter_ref, down_ref, chosen_ref):
    for r in range(chosen_ref.shape[0]):
        chosen_ref[r] = down_ref[adapter_ref[r]]


def fold_kernel(keep_ref, cores_ref, mine_ref, other_ref):
    quarter = mine_ref.shape[1] - HEAD
    core, z = lax.axis_index("core"), lax.axis_index("zl")
    for ref, which in ((other_ref, 1 - z), (mine_ref, z)):
        for cols, at in (
            (pl.ds(pl.multiple_of(which * quarter, quarter), quarter), pl.ds(0, quarter)),
            (pl.ds(NZ * quarter, HEAD), pl.ds(quarter, HEAD)),
        ):
            ref[:, at] = (keep_ref[:, cols] + cores_ref[1 - core, :, cols].astype(F32)).astype(ref.dtype)


def finish_kernel(lengths_ref, adapter_ref, mine_ref, other_ref, state_ref, gate_ref, up_ref, out_ref):
    rows, quarter = out_ref.shape
    reqs = lengths_ref.shape[0]
    ranks = up_ref.shape[1]
    seg = own_segments(rows, lengths_ref)
    there = 1 - lax.axis_index("zl")
    rank = mine_ref[:, quarter : quarter + HEAD] + other_ref[there, :, quarter : quarter + HEAD].astype(F32)
    rank = jnp.concatenate([rank] * (reqs * ranks // HEAD), axis=1)
    owner = lax.broadcasted_iota(jnp.int32, rank.shape, 1) // ranks
    rank = jnp.where(seg == owner, rank, 0.0).astype(BF16)
    ups = jnp.concatenate([up_ref[adapter_ref[r]] for r in range(reqs)], axis=0)
    gates = jnp.zeros((rows, quarter), F32)
    for r in range(reqs):
        gates = jnp.where(seg == r, gate_ref[r : r + 1, :], gates)
    branch = mine_ref[:, 0:quarter] + other_ref[there, :, 0:quarter].astype(F32)
    branch = branch + jnp.dot(rank, ups, preferred_element_type=F32)
    out_ref[...] = (state_ref[...].astype(F32) + gates * branch).astype(out_ref.dtype)


def shards(lengths, adapter, query, previous_keys, previous_values, stream, gate, output_matrix, adapter_down, adapter_up):
    rows, feats = query.shape[1:]
    quarter = output_matrix.shape[2] // (NZ * NC)
    group = NX * NYL
    smem = pl.BlockSpec(memory_space=pltpu.SMEM)
    vmem = pl.BlockSpec(memory_space=pltpu.VMEM)
    hbm = pl.BlockSpec(memory_space=pl.ANY)
    params = pltpu.CompilerParams(vmem_limit_bytes=VMEM_LIMIT)

    sections = lax.axis_size("section")
    state = lax.ppermute(stream[0], "section", [(i, (i + 1) % sections) for i in range(sections)])

    pair = lax.all_gather(query[0], "yl", axis=0, tiled=True)
    queries = pl.pallas_call(
        spread_kernel,
        in_specs=[vmem],
        out_specs=hbm,
        out_shape=jax.ShapeDtypeStruct((NX, NYL * rows, feats), BF16),
        scratch_shapes=[pltpu.SemaphoreType.DMA((NX,))],
        compiler_params=params,
    )(pair)
    kv = jnp.concatenate([previous_keys[0], previous_values[0]], axis=1)
    queries = lax.all_to_all(queries, "x", 0, 0, tiled=True)
    kv = lax.all_gather(kv, "yh", axis=0, tiled=True)

    keys = NYH * rows
    parts = pl.pallas_call(
        attend_kernel,
        in_specs=[smem, vmem, vmem],
        out_specs=hbm,
        out_shape=jax.ShapeDtypeStruct((group, feats + STAT_ROWS, rows), BF16),
        scratch_shapes=[
            pltpu.VMEM((feats, keys), BF16),
            pltpu.VMEM((group, feats + STAT_ROWS, rows), BF16),
            pltpu.SemaphoreType.DMA((feats // HEAD + 1,)),
        ],
        compiler_params=params,
    )(lengths, queries.reshape(group * rows, feats), kv)
    parts = lax.all_to_all(parts, ("x", "yl"), 0, 0, tiled=True, axis_index_groups=[ORDER])

    down = jnp.swapaxes(adapter_down[0], 1, 2)
    matrix = pl.pallas_call(
        hold_kernel,
        in_specs=[vmem],
        out_specs=vmem,
        out_shape=jax.ShapeDtypeStruct(output_matrix.shape[1:], BF16),
        compiler_params=params,
    )(output_matrix[0])
    down = pl.pallas_call(
        choose_kernel,
        in_specs=[smem, vmem],
        out_specs=vmem,
        out_shape=jax.ShapeDtypeStruct((adapter.shape[0],) + down.shape[1:], BF16),
        compiler_params=params,
    )(adapter, down)
    width = NZ * quarter + HEAD
    send, keep = pl.pallas_call(
        project_kernel,
        in_specs=[smem, vmem, vmem, vmem],
        out_specs=[vmem, vmem],
        out_shape=[jax.ShapeDtypeStruct((rows, width), BF16), jax.ShapeDtypeStruct((rows, width), F32)],
        compiler_params=params,
    )(lengths, parts, down, matrix)
    cores = lax.all_gather(send, "core", axis=0, tiled=False)
    mine, other = pl.pallas_call(
        fold_kernel,
        in_specs=[vmem, vmem],
        out_specs=[vmem, vmem],
        out_shape=[jax.ShapeDtypeStruct((rows, quarter + HEAD), F32), jax.ShapeDtypeStruct((rows, quarter + HEAD), BF16)],
        compiler_params=params,
    )(keep, cores)
    other = lax.all_gather(other, "zl", axis=0, tiled=False)

    out = pl.pallas_call(
        finish_kernel,
        in_specs=[smem, smem] + [vmem] * 5,
        out_specs=vmem,
        out_shape=jax.ShapeDtypeStruct((rows, quarter), BF16),
        compiler_params=params,
    )(lengths, adapter, mine, other, state, gate[0], adapter_up[0])
    return out[None]


def solution(mesh):
    devices = mesh.devices.reshape(mesh.shape["section"], NX, NYH, NYL, NZ, NC)
    fine = Mesh(devices, ("section", "x", "yh", "yl", "zl", "core"))
    seq, head = ("x", "yh", "yl"), ("zl", "core")
    placed = (
        P(),
        P(),
        P("section", seq, head),
        P("section", seq, head),
        P("section", seq, head),
        P("section", seq, head),
        P("section", None, head),
        P("section", head, None),
        P("section", None, head, None),
        P("section", None, None, head),
    )
    return jax.shard_map(shards, mesh=fine, in_specs=placed, out_specs=P("section", seq, head), check_vma=False)
```

```python
import functools
import math

import jax
import jax.numpy as jnp
from jax import lax
from jax.experimental import pallas as pl
from jax.experimental.pallas import tpu as pltpu
from jax.sharding import Mesh, PartitionSpec as P

HEAD = 128
NEG = -1e30
NX, NYH, NYL = 4, 4, 2
NZ, NC = 2, 2
STAT_ROWS = 16
ORDER = [0, 4, 2, 6, 1, 5, 3, 7]
F32 = jnp.float32
BF16 = jnp.bfloat16
VMEM_LIMIT = 16 * 1024 * 1024


def segment_of(position, lengths_ref):
    seg = jnp.zeros(position.shape, jnp.int32)
    end = 0
    for r in range(lengths_ref.shape[0]):
        end = end + lengths_ref[r]
        seg = seg + (position >= end).astype(jnp.int32)
    return seg


def spans(lengths_ref):
    lane = lax.broadcasted_iota(jnp.int32, (1, HEAD), 1)
    start = jnp.zeros((1, HEAD), jnp.int32)
    stop = jnp.full((1, HEAD), jnp.iinfo(jnp.int32).max, jnp.int32)
    end = 0
    for r in range(lengths_ref.shape[0]):
        start = jnp.where(lane == r, end, start)
        end = end + lengths_ref[r]
        stop = jnp.where(lane == r, end, stop)
    return start, stop


def own_segments(rows, lengths_ref):
    first = ((lax.axis_index("x") * NYH + lax.axis_index("yh")) * NYL + lax.axis_index("yl")) * rows
    return segment_of(first + lax.broadcasted_iota(jnp.int32, (rows, 1), 0), lengths_ref)


def spread_kernel(q_ref, out_ref, sems):
    copies = [pltpu.make_async_copy(q_ref, out_ref.at[i], sems.at[i]) for i in range(out_ref.shape[0])]
    for copy in copies:
        copy.start()
    for copy in copies:
        copy.wait()


def attend_kernel(lengths_ref, q_ref, kv_ref, result_ref, vt_ref, out_ref, sems):
    blocks, rows, feats = out_ref.shape[0], out_ref.shape[2], q_ref.shape[1]
    heads = feats // HEAD
    keys = kv_ref.shape[0]
    my_x, my_yh, my_yl = lax.axis_index("x"), lax.axis_index("yh"), lax.axis_index("yl")
    scale = math.log2(math.e) / math.sqrt(HEAD)

    start, stop = spans(lengths_ref)
    row = lax.broadcasted_iota(jnp.int32, (keys, HEAD), 0)
    block = row // rows
    place = ((my_x * NYH + block) * NYL + my_yl) * rows + (row - block * rows)
    bar = jnp.where((place >= start) & (place < stop), 0.0, NEG).astype(BF16)
    vt_ref[...] = kv_ref[:, feats : 2 * feats].T

    n_q = blocks * rows
    span = NYL * rows
    row = lax.broadcasted_iota(jnp.int32, (n_q, HEAD), 0)
    block = row // span
    place = (block * NYH + my_yh) * span + (row - block * span)
    member = jnp.where((place >= start) & (place < stop), 1.0, 0.0).astype(BF16)
    scores = []
    for h in range(heads):
        at = slice(h * HEAD, (h + 1) * HEAD)
        these = jnp.concatenate([kv_ref[:, at], bar], axis=1)
        queries = jnp.concatenate([q_ref[:, at], member], axis=1)
        scores.append(lax.dot_general(these, queries, (((1,), (1,)), ((), ())), preferred_element_type=F32))
    copies = []

    def send(start, size):
        at = (slice(None), pl.ds(start, size))
        copies.append(pltpu.make_async_copy(out_ref.at[at], result_ref.at[at], sems.at[len(copies)]))
        copies[-1].start()

    high, mid, low = [], [], []
    for h in range(heads):
        top = jnp.max(scores[h], axis=0, keepdims=True)
        weight = jnp.exp2((scores[h] - top) * scale)
        total = jnp.sum(weight, axis=0, keepdims=True)
        part = jnp.dot(vt_ref[h * HEAD : (h + 1) * HEAD, :], weight.astype(BF16), preferred_element_type=F32)
        part = (part * (1.0 / total)).astype(BF16)
        for i in range(blocks):
            out_ref[ORDER.index(i), h * HEAD : (h + 1) * HEAD, :] = part[:, i * rows : (i + 1) * rows]
        send(h * HEAD, HEAD)
        level = top * scale + jnp.log2(total)
        a = level.astype(BF16).astype(F32)
        b = (level - a).astype(BF16).astype(F32)
        high.append(a)
        mid.append(b)
        low.append(level - a - b)
    blank = [jnp.zeros((1, n_q), F32)] * (STAT_ROWS - 3 * heads)
    stats = jnp.concatenate(high + mid + low + blank, axis=0).astype(BF16)
    for i in range(blocks):
        out_ref[ORDER.index(i), feats : feats + STAT_ROWS, :] = stats[:, i * rows : (i + 1) * rows]
    send(feats, STAT_ROWS)
    for copy in copies:
        copy.wait()


def project_kernel(lengths_ref, part_ref, down_ref, w_ref, send_ref, keep_ref):
    groups = part_ref.shape[0]
    feats, out_feats = w_ref.shape
    rows = part_ref.shape[2]
    heads = feats // HEAD
    quarter = out_feats // (NZ * NC)
    stat = part_ref[:, feats : feats + STAT_ROWS, :].astype(F32)
    level = stat[:, 0:heads] + stat[:, heads : 2 * heads] + stat[:, 2 * heads : 3 * heads]
    share = jnp.exp2(level - jnp.max(level, axis=0, keepdims=True))
    share = share / jnp.sum(share, axis=0, keepdims=True)
    columns = []
    for h in range(heads):
        acc = jnp.zeros((HEAD, rows), F32)
        for g in range(groups):
            acc = acc + part_ref[g, h * HEAD : (h + 1) * HEAD, :].astype(F32) * share[g, h : h + 1, :]
        columns.append(acc.T.astype(BF16))
    attn = jnp.concatenate(columns, axis=1)

    seg = own_segments(rows, lengths_ref)
    rank = jnp.zeros((rows, down_ref.shape[1]), F32)
    for r in range(lengths_ref.shape[0]):
        mid = lax.dot_general(attn, down_ref[r], (((1,), (1,)), ((), ())), preferred_element_type=F32)
        rank = rank + jnp.where(seg == r, mid, 0.0)
    rank = jnp.concatenate([rank] * (HEAD // rank.shape[1]), axis=1)
    core = lax.axis_index("core")
    for z in range(NZ):
        for ref, c in ((send_ref, 1 - core), (keep_ref, core)):
            start = pl.multiple_of((z * NC + c) * quarter, quarter)
            product = jnp.dot(attn, w_ref[:, pl.ds(start, quarter)], preferred_element_type=F32)
            ref[:, z * quarter : (z + 1) * quarter] = product.astype(ref.dtype)
    send_ref[:, NZ * quarter : NZ * quarter + HEAD] = rank.astype(send_ref.dtype)
    keep_ref[:, NZ * quarter : NZ * quarter + HEAD] = rank.astype(keep_ref.dtype)


def hold_kernel(matrix_ref, w_ref):
    w_ref[...] = matrix_ref[...]


def choose_kernel(adapter_ref, down_ref, chosen_ref):
    for r in range(chosen_ref.shape[0]):
        chosen_ref[r] = down_ref[adapter_ref[r]]


def fold_kernel(keep_ref, cores_ref, mine_ref, other_ref):
    quarter = mine_ref.shape[1] - HEAD
    core, z = lax.axis_index("core"), lax.axis_index("zl")
    for ref, which in ((other_ref, 1 - z), (mine_ref, z)):
        for cols, at in (
            (pl.ds(pl.multiple_of(which * quarter, quarter), quarter), pl.ds(0, quarter)),
            (pl.ds(NZ * quarter, HEAD), pl.ds(quarter, HEAD)),
        ):
            ref[:, at] = (keep_ref[:, cols].astype(F32) + cores_ref[1 - core, :, cols].astype(F32)).astype(ref.dtype)


def finish_kernel(lengths_ref, adapter_ref, mine_ref, other_ref, state_ref, gate_ref, up_ref, out_ref):
    rows, quarter = out_ref.shape
    reqs = lengths_ref.shape[0]
    ranks = up_ref.shape[1]
    seg = own_segments(rows, lengths_ref)
    there = 1 - lax.axis_index("zl")
    rank = mine_ref[:, quarter : quarter + HEAD] + other_ref[there, :, quarter : quarter + HEAD].astype(F32)
    rank = jnp.concatenate([rank] * (reqs * ranks // HEAD), axis=1)
    owner = lax.broadcasted_iota(jnp.int32, rank.shape, 1) // ranks
    rank = jnp.where(seg == owner, rank, 0.0).astype(BF16)
    ups = jnp.concatenate([up_ref[adapter_ref[r]] for r in range(reqs)], axis=0)
    gates = jnp.zeros((rows, quarter), F32)
    for r in range(reqs):
        gates = jnp.where(seg == r, gate_ref[r : r + 1, :], gates)
    branch = mine_ref[:, 0:quarter] + other_ref[there, :, 0:quarter].astype(F32)
    branch = branch + jnp.dot(rank, ups, preferred_element_type=F32)
    out_ref[...] = (state_ref[...].astype(F32) + gates * branch).astype(out_ref.dtype)


def shards(lengths, adapter, query, previous_keys, previous_values, stream, gate, output_matrix, adapter_down, adapter_up):
    rows, feats = query.shape[1:]
    quarter = output_matrix.shape[2] // (NZ * NC)
    group = NX * NYL
    smem = pl.BlockSpec(memory_space=pltpu.SMEM)
    vmem = pl.BlockSpec(memory_space=pltpu.VMEM)
    hbm = pl.BlockSpec(memory_space=pl.ANY)
    params = pltpu.CompilerParams(vmem_limit_bytes=VMEM_LIMIT)

    sections = lax.axis_size("section")
    state = lax.ppermute(stream[0], "section", [(i, (i + 1) % sections) for i in range(sections)])

    pair = lax.all_gather(query[0], "yl", axis=0, tiled=True)
    queries = pl.pallas_call(
        spread_kernel,
        in_specs=[vmem],
        out_specs=hbm,
        out_shape=jax.ShapeDtypeStruct((NX, NYL * rows, feats), BF16),
        scratch_shapes=[pltpu.SemaphoreType.DMA((NX,))],
        compiler_params=params,
    )(pair)
    kv = jnp.concatenate([previous_keys[0], previous_values[0]], axis=1)
    queries = lax.all_to_all(queries, "x", 0, 0, tiled=True)
    kv = lax.all_gather(kv, "yh", axis=0, tiled=True)

    keys = NYH * rows
    parts = pl.pallas_call(
        attend_kernel,
        in_specs=[smem, vmem, vmem],
        out_specs=hbm,
        out_shape=jax.ShapeDtypeStruct((group, feats + STAT_ROWS, rows), BF16),
        scratch_shapes=[
            pltpu.VMEM((feats, keys), BF16),
            pltpu.VMEM((group, feats + STAT_ROWS, rows), BF16),
            pltpu.SemaphoreType.DMA((feats // HEAD + 1,)),
        ],
        compiler_params=params,
    )(lengths, queries.reshape(group * rows, feats), kv)
    parts = lax.all_to_all(parts, ("x", "yl"), 0, 0, tiled=True, axis_index_groups=[ORDER])

    down = jnp.swapaxes(adapter_down[0], 1, 2)
    matrix = pl.pallas_call(
        hold_kernel,
        in_specs=[vmem],
        out_specs=vmem,
        out_shape=jax.ShapeDtypeStruct(output_matrix.shape[1:], BF16),
        compiler_params=params,
    )(output_matrix[0])
    down = pl.pallas_call(
        choose_kernel,
        in_specs=[smem, vmem],
        out_specs=vmem,
        out_shape=jax.ShapeDtypeStruct((adapter.shape[0],) + down.shape[1:], BF16),
        compiler_params=params,
    )(adapter, down)
    width = NZ * quarter + HEAD
    send, keep = pl.pallas_call(
        project_kernel,
        in_specs=[smem, vmem, vmem, vmem],
        out_specs=[vmem, vmem],
        out_shape=[jax.ShapeDtypeStruct((rows, width), BF16), jax.ShapeDtypeStruct((rows, width), BF16)],
        compiler_params=params,
    )(lengths, parts, down, matrix)
    cores = lax.all_gather(send, "core", axis=0, tiled=False)
    mine, other = pl.pallas_call(
        fold_kernel,
        in_specs=[vmem, vmem],
        out_specs=[vmem, vmem],
        out_shape=[jax.ShapeDtypeStruct((rows, quarter + HEAD), F32), jax.ShapeDtypeStruct((rows, quarter + HEAD), BF16)],
        compiler_params=params,
    )(keep, cores)
    other = lax.all_gather(other, "zl", axis=0, tiled=False)

    out = pl.pallas_call(
        finish_kernel,
        in_specs=[smem, smem] + [vmem] * 5,
        out_specs=vmem,
        out_shape=jax.ShapeDtypeStruct((rows, quarter), BF16),
        compiler_params=params,
    )(lengths, adapter, mine, other, state, gate[0], adapter_up[0])
    return out[None]


def solution(mesh):
    devices = mesh.devices.reshape(mesh.shape["section"], NX, NYH, NYL, NZ, NC)
    fine = Mesh(devices, ("section", "x", "yh", "yl", "zl", "core"))
    seq, head = ("x", "yh", "yl"), ("zl", "core")
    placed = (
        P(),
        P(),
        P("section", seq, head),
        P("section", seq, head),
        P("section", seq, head),
        P("section", seq, head),
        P("section", None, head),
        P("section", head, None),
        P("section", None, head, None),
        P("section", None, None, head),
    )
    return jax.shard_map(shards, mesh=fine, in_specs=placed, out_specs=P("section", seq, head), check_vma=False)
```

```python
import functools
import math

import jax
import jax.numpy as jnp
from jax import lax
from jax.experimental import pallas as pl
from jax.experimental.pallas import tpu as pltpu
from jax.sharding import Mesh, PartitionSpec as P

HEAD = 128
NEG = -1e30
NX, NYH, NYL = 4, 4, 2
NZ, NC = 2, 2
STAT_ROWS = 16
ORDER = [0, 4, 2, 6, 1, 5, 3, 7]
F32 = jnp.float32
BF16 = jnp.bfloat16
VMEM_LIMIT = 16 * 1024 * 1024


def segment_of(position, lengths_ref):
    seg = jnp.zeros(position.shape, jnp.int32)
    end = 0
    for r in range(lengths_ref.shape[0]):
        end = end + lengths_ref[r]
        seg = seg + (position >= end).astype(jnp.int32)
    return seg


def spans(lengths_ref):
    lane = lax.broadcasted_iota(jnp.int32, (1, HEAD), 1)
    start = jnp.zeros((1, HEAD), jnp.int32)
    stop = jnp.full((1, HEAD), jnp.iinfo(jnp.int32).max, jnp.int32)
    end = 0
    for r in range(lengths_ref.shape[0]):
        start = jnp.where(lane == r, end, start)
        end = end + lengths_ref[r]
        stop = jnp.where(lane == r, end, stop)
    return start, stop


def own_segments(rows, lengths_ref):
    first = ((lax.axis_index("x") * NYH + lax.axis_index("yh")) * NYL + lax.axis_index("yl")) * rows
    return segment_of(first + lax.broadcasted_iota(jnp.int32, (rows, 1), 0), lengths_ref)


def spread_kernel(q_ref, out_ref, sems):
    copies = [pltpu.make_async_copy(q_ref, out_ref.at[i], sems.at[i]) for i in range(out_ref.shape[0])]
    for copy in copies:
        copy.start()
    for copy in copies:
        copy.wait()


def attend_kernel(lengths_ref, q_ref, kv_ref, result_ref, vt_ref, out_ref, sems):
    blocks, rows, feats = out_ref.shape[0], out_ref.shape[2], q_ref.shape[1]
    heads = feats // HEAD
    keys = kv_ref.shape[0]
    my_x, my_yh, my_yl = lax.axis_index("x"), lax.axis_index("yh"), lax.axis_index("yl")
    scale = math.log2(math.e) / math.sqrt(HEAD)

    start, stop = spans(lengths_ref)
    row = lax.broadcasted_iota(jnp.int32, (keys, HEAD), 0)
    block = row // rows
    place = ((my_x * NYH + block) * NYL + my_yl) * rows + (row - block * rows)
    bar = jnp.where((place >= start) & (place < stop), 0.0, NEG).astype(BF16)
    vt_ref[...] = kv_ref[:, feats : 2 * feats].T

    n_q = blocks * rows
    span = NYL * rows
    row = lax.broadcasted_iota(jnp.int32, (n_q, HEAD), 0)
    block = row // span
    place = (block * NYH + my_yh) * span + (row - block * span)
    member = jnp.where((place >= start) & (place < stop), 1.0, 0.0).astype(BF16)
    scores = []
    for h in range(heads):
        at = slice(h * HEAD, (h + 1) * HEAD)
        these = jnp.concatenate([kv_ref[:, at], bar], axis=1)
        queries = jnp.concatenate([q_ref[:, at], member], axis=1)
        scores.append(lax.dot_general(these, queries, (((1,), (1,)), ((), ())), preferred_element_type=F32))
    copies = []

    def send(start, size):
        at = (slice(None), pl.ds(start, size))
        copies.append(pltpu.make_async_copy(out_ref.at[at], result_ref.at[at], sems.at[len(copies)]))
        copies[-1].start()

    high, mid, low = [], [], []
    for h in range(heads):
        top = jnp.max(scores[h], axis=0, keepdims=True)
        weight = jnp.exp2((scores[h] - top) * scale)
        total = jnp.sum(weight, axis=0, keepdims=True)
        part = jnp.dot(vt_ref[h * HEAD : (h + 1) * HEAD, :], weight.astype(BF16), preferred_element_type=F32)
        part = (part * (1.0 / total)).astype(BF16)
        for i in range(blocks):
            out_ref[ORDER.index(i), h * HEAD : (h + 1) * HEAD, :] = part[:, i * rows : (i + 1) * rows]
        send(h * HEAD, HEAD)
        level = top * scale + jnp.log2(total)
        a = level.astype(BF16).astype(F32)
        b = (level - a).astype(BF16).astype(F32)
        high.append(a)
        mid.append(b)
        low.append(level - a - b)
    blank = [jnp.zeros((1, n_q), F32)] * (STAT_ROWS - 3 * heads)
    stats = jnp.concatenate(high + mid + low + blank, axis=0).astype(BF16)
    for i in range(blocks):
        out_ref[ORDER.index(i), feats : feats + STAT_ROWS, :] = stats[:, i * rows : (i + 1) * rows]
    send(feats, STAT_ROWS)
    for copy in copies:
        copy.wait()


def project_kernel(lengths_ref, part_ref, down_ref, w_ref, send_ref, keep_ref):
    groups = part_ref.shape[0]
    feats, out_feats = w_ref.shape
    rows = part_ref.shape[2]
    heads = feats // HEAD
    quarter = out_feats // (NZ * NC)
    stat = part_ref[:, feats : feats + STAT_ROWS, :].astype(F32)
    level = stat[:, 0:heads] + stat[:, heads : 2 * heads] + stat[:, 2 * heads : 3 * heads]
    share = jnp.exp2(level - jnp.max(level, axis=0, keepdims=True))
    share = share / jnp.sum(share, axis=0, keepdims=True)
    columns = []
    for h in range(heads):
        acc = jnp.zeros((HEAD, rows), F32)
        for g in range(groups):
            acc = acc + part_ref[g, h * HEAD : (h + 1) * HEAD, :].astype(F32) * share[g, h : h + 1, :]
        columns.append(acc.T.astype(BF16))
    attn = jnp.concatenate(columns, axis=1)

    seg = own_segments(rows, lengths_ref)
    rank = jnp.zeros((rows, down_ref.shape[1]), F32)
    for r in range(lengths_ref.shape[0]):
        mid = lax.dot_general(attn, down_ref[r], (((1,), (1,)), ((), ())), preferred_element_type=F32)
        rank = rank + jnp.where(seg == r, mid, 0.0)
    rank = jnp.concatenate([rank] * (HEAD // rank.shape[1]), axis=1)
    core = lax.axis_index("core")
    for z in range(NZ):
        for ref, c in ((send_ref, 1 - core), (keep_ref, core)):
            start = pl.multiple_of((z * NC + c) * quarter, quarter)
            product = jnp.dot(attn, w_ref[:, pl.ds(start, quarter)], preferred_element_type=F32)
            ref[:, z * quarter : (z + 1) * quarter] = product.astype(ref.dtype)
    send_ref[:, NZ * quarter : NZ * quarter + HEAD] = rank.astype(send_ref.dtype)
    keep_ref[:, NZ * quarter : NZ * quarter + HEAD] = rank.astype(keep_ref.dtype)


def hold_kernel(matrix_ref, w_ref):
    w_ref[...] = matrix_ref[...]


def choose_kernel(adapter_ref, down_ref, chosen_ref):
    for r in range(chosen_ref.shape[0]):
        chosen_ref[r] = down_ref[adapter_ref[r]]


def fold_kernel(keep_ref, cores_ref, mine_ref, other_ref):
    quarter = mine_ref.shape[1] - HEAD
    core, z = lax.axis_index("core"), lax.axis_index("zl")
    for ref, which in ((other_ref, 1 - z), (mine_ref, z)):
        for cols, at in (
            (pl.ds(pl.multiple_of(which * quarter, quarter), quarter), pl.ds(0, quarter)),
            (pl.ds(NZ * quarter, HEAD), pl.ds(quarter, HEAD)),
        ):
            ref[:, at] = (keep_ref[:, cols].astype(F32) + cores_ref[1 - core, :, cols].astype(F32)).astype(ref.dtype)


def finish_kernel(lengths_ref, adapter_ref, mine_ref, other_ref, state_ref, gate_ref, up_ref, out_ref):
    rows, quarter = out_ref.shape
    reqs = lengths_ref.shape[0]
    ranks = up_ref.shape[1]
    seg = own_segments(rows, lengths_ref)
    there = 1 - lax.axis_index("zl")
    rank = mine_ref[:, quarter : quarter + HEAD].astype(F32) + other_ref[there, :, quarter : quarter + HEAD].astype(F32)
    rank = jnp.concatenate([rank] * (reqs * ranks // HEAD), axis=1)
    owner = lax.broadcasted_iota(jnp.int32, rank.shape, 1) // ranks
    rank = jnp.where(seg == owner, rank, 0.0).astype(BF16)
    ups = jnp.concatenate([up_ref[adapter_ref[r]] for r in range(reqs)], axis=0)
    gates = jnp.zeros((rows, quarter), F32)
    for r in range(reqs):
        gates = jnp.where(seg == r, gate_ref[r : r + 1, :], gates)
    branch = mine_ref[:, 0:quarter].astype(F32) + other_ref[there, :, 0:quarter].astype(F32)
    branch = branch + jnp.dot(rank, ups, preferred_element_type=F32)
    out_ref[...] = (state_ref[...].astype(F32) + gates * branch).astype(out_ref.dtype)


def shards(lengths, adapter, query, previous_keys, previous_values, stream, gate, output_matrix, adapter_down, adapter_up):
    rows, feats = query.shape[1:]
    quarter = output_matrix.shape[2] // (NZ * NC)
    group = NX * NYL
    smem = pl.BlockSpec(memory_space=pltpu.SMEM)
    vmem = pl.BlockSpec(memory_space=pltpu.VMEM)
    hbm = pl.BlockSpec(memory_space=pl.ANY)
    params = pltpu.CompilerParams(vmem_limit_bytes=VMEM_LIMIT)

    sections = lax.axis_size("section")
    state = lax.ppermute(stream[0], "section", [(i, (i + 1) % sections) for i in range(sections)])

    pair = lax.all_gather(query[0], "yl", axis=0, tiled=True)
    queries = pl.pallas_call(
        spread_kernel,
        in_specs=[vmem],
        out_specs=hbm,
        out_shape=jax.ShapeDtypeStruct((NX, NYL * rows, feats), BF16),
        scratch_shapes=[pltpu.SemaphoreType.DMA((NX,))],
        compiler_params=params,
    )(pair)
    kv = jnp.concatenate([previous_keys[0], previous_values[0]], axis=1)
    queries = lax.all_to_all(queries, "x", 0, 0, tiled=True)
    kv = lax.all_gather(kv, "yh", axis=0, tiled=True)

    keys = NYH * rows
    parts = pl.pallas_call(
        attend_kernel,
        in_specs=[smem, vmem, vmem],
        out_specs=hbm,
        out_shape=jax.ShapeDtypeStruct((group, feats + STAT_ROWS, rows), BF16),
        scratch_shapes=[
            pltpu.VMEM((feats, keys), BF16),
            pltpu.VMEM((group, feats + STAT_ROWS, rows), BF16),
            pltpu.SemaphoreType.DMA((feats // HEAD + 1,)),
        ],
        compiler_params=params,
    )(lengths, queries.reshape(group * rows, feats), kv)
    parts = lax.all_to_all(parts, ("x", "yl"), 0, 0, tiled=True, axis_index_groups=[ORDER])

    down = jnp.swapaxes(adapter_down[0], 1, 2)
    matrix = pl.pallas_call(
        hold_kernel,
        in_specs=[vmem],
        out_specs=vmem,
        out_shape=jax.ShapeDtypeStruct(output_matrix.shape[1:], BF16),
        compiler_params=params,
    )(output_matrix[0])
    down = pl.pallas_call(
        choose_kernel,
        in_specs=[smem, vmem],
        out_specs=vmem,
        out_shape=jax.ShapeDtypeStruct((adapter.shape[0],) + down.shape[1:], BF16),
        compiler_params=params,
    )(adapter, down)
    width = NZ * quarter + HEAD
    send, keep = pl.pallas_call(
        project_kernel,
        in_specs=[smem, vmem, vmem, vmem],
        out_specs=[vmem, vmem],
        out_shape=[jax.ShapeDtypeStruct((rows, width), BF16), jax.ShapeDtypeStruct((rows, width), BF16)],
        compiler_params=params,
    )(lengths, parts, down, matrix)
    cores = lax.all_gather(send, "core", axis=0, tiled=False)
    mine, other = pl.pallas_call(
        fold_kernel,
        in_specs=[vmem, vmem],
        out_specs=[vmem, vmem],
        out_shape=[jax.ShapeDtypeStruct((rows, quarter + HEAD), BF16)] * 2,
        compiler_params=params,
    )(keep, cores)
    other = lax.all_gather(other, "zl", axis=0, tiled=False)

    out = pl.pallas_call(
        finish_kernel,
        in_specs=[smem, smem] + [vmem] * 5,
        out_specs=vmem,
        out_shape=jax.ShapeDtypeStruct((rows, quarter), BF16),
        compiler_params=params,
    )(lengths, adapter, mine, other, state, gate[0], adapter_up[0])
    return out[None]


def solution(mesh):
    devices = mesh.devices.reshape(mesh.shape["section"], NX, NYH, NYL, NZ, NC)
    fine = Mesh(devices, ("section", "x", "yh", "yl", "zl", "core"))
    seq, head = ("x", "yh", "yl"), ("zl", "core")
    placed = (
        P(),
        P(),
        P("section", seq, head),
        P("section", seq, head),
        P("section", seq, head),
        P("section", seq, head),
        P("section", None, head),
        P("section", head, None),
        P("section", None, head, None),
        P("section", None, None, head),
    )
    return jax.shard_map(shards, mesh=fine, in_specs=placed, out_specs=P("section", seq, head), check_vma=False)
```

```python
import functools
import math

import jax
import jax.numpy as jnp
from jax import lax
from jax.experimental import pallas as pl
from jax.experimental.pallas import tpu as pltpu
from jax.sharding import Mesh, PartitionSpec as P

HEAD = 128
NEG = -1e30
NX, NYH, NYL = 4, 4, 2
NZ, NC = 2, 2
STAT_ROWS = 16
ORDER = [0, 5, 1, 4, 2, 7, 3, 6]
F32 = jnp.float32
BF16 = jnp.bfloat16
VMEM_LIMIT = 16 * 1024 * 1024


def segment_of(position, lengths_ref):
    seg = jnp.zeros(position.shape, jnp.int32)
    end = 0
    for r in range(lengths_ref.shape[0]):
        end = end + lengths_ref[r]
        seg = seg + (position >= end).astype(jnp.int32)
    return seg


def spans(lengths_ref):
    lane = lax.broadcasted_iota(jnp.int32, (1, HEAD), 1)
    start = jnp.zeros((1, HEAD), jnp.int32)
    stop = jnp.full((1, HEAD), jnp.iinfo(jnp.int32).max, jnp.int32)
    end = 0
    for r in range(lengths_ref.shape[0]):
        start = jnp.where(lane == r, end, start)
        end = end + lengths_ref[r]
        stop = jnp.where(lane == r, end, stop)
    return start, stop


def own_segments(rows, lengths_ref):
    first = ((lax.axis_index("x") * NYH + lax.axis_index("yh")) * NYL + lax.axis_index("yl")) * rows
    return segment_of(first + lax.broadcasted_iota(jnp.int32, (rows, 1), 0), lengths_ref)


def spread_kernel(q_ref, out_ref, sems):
    copies = [pltpu.make_async_copy(q_ref, out_ref.at[i], sems.at[i]) for i in range(out_ref.shape[0])]
    for copy in copies:
        copy.start()
    for copy in copies:
        copy.wait()


def attend_kernel(lengths_ref, q_ref, kv_ref, result_ref, vt_ref, out_ref, sems):
    blocks, rows, feats = out_ref.shape[0], out_ref.shape[2], q_ref.shape[1]
    heads = feats // HEAD
    keys = kv_ref.shape[0]
    my_x, my_yh, my_yl = lax.axis_index("x"), lax.axis_index("yh"), lax.axis_index("yl")
    scale = math.log2(math.e) / math.sqrt(HEAD)

    start, stop = spans(lengths_ref)
    row = lax.broadcasted_iota(jnp.int32, (keys, HEAD), 0)
    block = row // rows
    place = ((my_x * NYH + block) * NYL + my_yl) * rows + (row - block * rows)
    bar = jnp.where((place >= start) & (place < stop), 0.0, NEG).astype(BF16)
    vt_ref[...] = kv_ref[:, feats : 2 * feats].T

    n_q = blocks * rows
    span = NYL * rows
    row = lax.broadcasted_iota(jnp.int32, (n_q, HEAD), 0)
    block = row // span
    place = (block * NYH + my_yh) * span + (row - block * span)
    member = jnp.where((place >= start) & (place < stop), 1.0, 0.0).astype(BF16)
    scores = []
    for h in range(heads):
        at = slice(h * HEAD, (h + 1) * HEAD)
        these = jnp.concatenate([kv_ref[:, at], bar], axis=1)
        queries = jnp.concatenate([q_ref[:, at], member], axis=1)
        scores.append(lax.dot_general(these, queries, (((1,), (1,)), ((), ())), preferred_element_type=F32))
    copies = []

    def send(start, size):
        at = (slice(None), pl.ds(start, size))
        copies.append(pltpu.make_async_copy(out_ref.at[at], result_ref.at[at], sems.at[len(copies)]))
        copies[-1].start()

    high, mid, low = [], [], []
    for h in range(heads):
        top = jnp.max(scores[h], axis=0, keepdims=True)
        weight = jnp.exp2((scores[h] - top) * scale)
        total = jnp.sum(weight, axis=0, keepdims=True)
        part = jnp.dot(vt_ref[h * HEAD : (h + 1) * HEAD, :], weight.astype(BF16), preferred_element_type=F32)
        part = (part * (1.0 / total)).astype(BF16)
        for i in range(blocks):
            out_ref[ORDER.index(i), h * HEAD : (h + 1) * HEAD, :] = part[:, i * rows : (i + 1) * rows]
        send(h * HEAD, HEAD)
        level = top * scale + jnp.log2(total)
        a = level.astype(BF16).astype(F32)
        b = (level - a).astype(BF16).astype(F32)
        high.append(a)
        mid.append(b)
        low.append(level - a - b)
    blank = [jnp.zeros((1, n_q), F32)] * (STAT_ROWS - 3 * heads)
    stats = jnp.concatenate(high + mid + low + blank, axis=0).astype(BF16)
    for i in range(blocks):
        out_ref[ORDER.index(i), feats : feats + STAT_ROWS, :] = stats[:, i * rows : (i + 1) * rows]
    send(feats, STAT_ROWS)
    for copy in copies:
        copy.wait()


def project_kernel(lengths_ref, part_ref, down_ref, w_ref, send_ref, keep_ref):
    groups = part_ref.shape[0]
    feats, out_feats = w_ref.shape
    rows = part_ref.shape[2]
    heads = feats // HEAD
    quarter = out_feats // (NZ * NC)
    stat = part_ref[:, feats : feats + STAT_ROWS, :].astype(F32)
    level = stat[:, 0:heads] + stat[:, heads : 2 * heads] + stat[:, 2 * heads : 3 * heads]
    share = jnp.exp2(level - jnp.max(level, axis=0, keepdims=True))
    share = share / jnp.sum(share, axis=0, keepdims=True)
    columns = []
    for h in range(heads):
        acc = jnp.zeros((HEAD, rows), F32)
        for g in range(groups):
            acc = acc + part_ref[g, h * HEAD : (h + 1) * HEAD, :].astype(F32) * share[g, h : h + 1, :]
        columns.append(acc.T.astype(BF16))
    attn = jnp.concatenate(columns, axis=1)

    seg = own_segments(rows, lengths_ref)
    rank = jnp.zeros((rows, down_ref.shape[1]), F32)
    for r in range(lengths_ref.shape[0]):
        mid = lax.dot_general(attn, down_ref[r], (((1,), (1,)), ((), ())), preferred_element_type=F32)
        rank = rank + jnp.where(seg == r, mid, 0.0)
    rank = jnp.concatenate([rank] * (HEAD // rank.shape[1]), axis=1)
    core = lax.axis_index("core")
    for z in range(NZ):
        for ref, c in ((send_ref, 1 - core), (keep_ref, core)):
            start = pl.multiple_of((z * NC + c) * quarter, quarter)
            product = jnp.dot(attn, w_ref[:, pl.ds(start, quarter)], preferred_element_type=F32)
            ref[:, z * quarter : (z + 1) * quarter] = product.astype(ref.dtype)
    send_ref[:, NZ * quarter : NZ * quarter + HEAD] = rank.astype(send_ref.dtype)
    keep_ref[:, NZ * quarter : NZ * quarter + HEAD] = rank.astype(keep_ref.dtype)


def hold_kernel(adapter_ref, matrix_ref, down_ref, w_ref, chosen_ref):
    w_ref[...] = matrix_ref[...]
    for r in range(chosen_ref.shape[0]):
        chosen_ref[r] = down_ref[adapter_ref[r]]


def fold_kernel(keep_ref, cores_ref, mine_ref, other_ref):
    quarter = mine_ref.shape[1] - HEAD
    core, z = lax.axis_index("core"), lax.axis_index("zl")
    for ref, which in ((other_ref, 1 - z), (mine_ref, z)):
        for cols, at in (
            (pl.ds(pl.multiple_of(which * quarter, quarter), quarter), pl.ds(0, quarter)),
            (pl.ds(NZ * quarter, HEAD), pl.ds(quarter, HEAD)),
        ):
            ref[:, at] = (keep_ref[:, cols] + cores_ref[1 - core, :, cols].astype(F32)).astype(ref.dtype)


def finish_kernel(lengths_ref, adapter_ref, mine_ref, other_ref, state_ref, gate_ref, up_ref, out_ref):
    rows, quarter = out_ref.shape
    reqs = lengths_ref.shape[0]
    ranks = up_ref.shape[1]
    seg = own_segments(rows, lengths_ref)
    there = 1 - lax.axis_index("zl")
    rank = mine_ref[:, quarter : quarter + HEAD] + other_ref[there, :, quarter : quarter + HEAD].astype(F32)
    rank = jnp.concatenate([rank] * (reqs * ranks // HEAD), axis=1)
    owner = lax.broadcasted_iota(jnp.int32, rank.shape, 1) // ranks
    rank = jnp.where(seg == owner, rank, 0.0).astype(BF16)
    ups = jnp.concatenate([up_ref[adapter_ref[r]] for r in range(reqs)], axis=0)
    gates = jnp.zeros((rows, quarter), F32)
    for r in range(reqs):
        gates = jnp.where(seg == r, gate_ref[r : r + 1, :], gates)
    branch = mine_ref[:, 0:quarter] + other_ref[there, :, 0:quarter].astype(F32)
    branch = branch + jnp.dot(rank, ups, preferred_element_type=F32)
    out_ref[...] = (state_ref[...].astype(F32) + gates * branch).astype(out_ref.dtype)


def shards(lengths, adapter, query, previous_keys, previous_values, stream, gate, output_matrix, adapter_down, adapter_up):
    rows, feats = query.shape[1:]
    quarter = output_matrix.shape[2] // (NZ * NC)
    group = NX * NYL
    smem = pl.BlockSpec(memory_space=pltpu.SMEM)
    vmem = pl.BlockSpec(memory_space=pltpu.VMEM)
    hbm = pl.BlockSpec(memory_space=pl.ANY)
    params = pltpu.CompilerParams(vmem_limit_bytes=VMEM_LIMIT)

    sections = lax.axis_size("section")
    state = lax.ppermute(stream[0], "section", [(i, (i + 1) % sections) for i in range(sections)])

    pair = lax.all_gather(query[0], "yl", axis=0, tiled=True)
    queries = pl.pallas_call(
        spread_kernel,
        in_specs=[vmem],
        out_specs=hbm,
        out_shape=jax.ShapeDtypeStruct((NX, NYL * rows, feats), BF16),
        scratch_shapes=[pltpu.SemaphoreType.DMA((NX,))],
        compiler_params=params,
    )(pair)
    kv = jnp.concatenate([previous_keys[0], previous_values[0]], axis=1)
    queries = lax.all_to_all(queries, "x", 0, 0, tiled=True)
    kv = lax.all_gather(kv, "yh", axis=0, tiled=True)

    keys = NYH * rows
    parts = pl.pallas_call(
        attend_kernel,
        in_specs=[smem, vmem, vmem],
        out_specs=hbm,
        out_shape=jax.ShapeDtypeStruct((group, feats + STAT_ROWS, rows), BF16),
        scratch_shapes=[
            pltpu.VMEM((feats, keys), BF16),
            pltpu.VMEM((group, feats + STAT_ROWS, rows), BF16),
            pltpu.SemaphoreType.DMA((feats // HEAD + 1,)),
        ],
        compiler_params=params,
    )(lengths, queries.reshape(group * rows, feats), kv)
    parts = lax.all_to_all(parts, ("x", "yl"), 0, 0, tiled=True, axis_index_groups=[ORDER])

    down = jnp.swapaxes(adapter_down[0], 1, 2)
    matrix, down = pl.pallas_call(
        hold_kernel,
        in_specs=[smem, vmem, vmem],
        out_specs=[vmem, vmem],
        out_shape=[
            jax.ShapeDtypeStruct(output_matrix.shape[1:], BF16),
            jax.ShapeDtypeStruct((adapter.shape[0],) + down.shape[1:], BF16),
        ],
        compiler_params=pltpu.CompilerParams(vmem_limit_bytes=VMEM_LIMIT),
    )(adapter, output_matrix[0], down)
    width = NZ * quarter + HEAD
    send, keep = pl.pallas_call(
        project_kernel,
        in_specs=[smem, vmem, vmem, vmem],
        out_specs=[vmem, vmem],
        out_shape=[jax.ShapeDtypeStruct((rows, width), BF16), jax.ShapeDtypeStruct((rows, width), F32)],
        compiler_params=params,
    )(lengths, parts, down, matrix)
    cores = lax.all_gather(send, "core", axis=0, tiled=False)
    mine, other = pl.pallas_call(
        fold_kernel,
        in_specs=[vmem, vmem],
        out_specs=[vmem, vmem],
        out_shape=[jax.ShapeDtypeStruct((rows, quarter + HEAD), F32), jax.ShapeDtypeStruct((rows, quarter + HEAD), BF16)],
        compiler_params=params,
    )(keep, cores)
    other = lax.all_gather(other, "zl", axis=0, tiled=False)

    out = pl.pallas_call(
        finish_kernel,
        in_specs=[smem, smem] + [vmem] * 5,
        out_specs=vmem,
        out_shape=jax.ShapeDtypeStruct((rows, quarter), BF16),
        compiler_params=params,
    )(lengths, adapter, mine, other, state, gate[0], adapter_up[0])
    return out[None]


def solution(mesh):
    devices = mesh.devices.reshape(mesh.shape["section"], NX, NYH, NYL, NZ, NC)
    fine = Mesh(devices, ("section", "x", "yh", "yl", "zl", "core"))
    seq, head = ("x", "yh", "yl"), ("zl", "core")
    placed = (
        P(),
        P(),
        P("section", seq, head),
        P("section", seq, head),
        P("section", seq, head),
        P("section", seq, head),
        P("section", None, head),
        P("section", head, None),
        P("section", None, head, None),
        P("section", None, None, head),
    )
    return jax.shard_map(shards, mesh=fine, in_specs=placed, out_specs=P("section", seq, head), check_vma=False)
```
